256 devices in a mesh: tile: 16 (over x_hi, z), map: 8 (over y, core), dp: 2 (over x_lo).
Axes of the slice: x: 4 (x_hi: 2, x_lo: 2; x = x_hi * 2 + x_lo), y: 4, z: 8, core: 2. Of those that a mesh axis runs over, the one named last changes fastest.
Arguments:
- frames: bfloat16 [3, 320, 128, 768], P(None, 'tile', None, 'dp'), may hold values from -6 to 6
- weights: bfloat16 [128, 972, 1024], P('tile', None, 'map'), may hold values from -0.1875 to 0.1875
- offsets: int32 [128, 2], P('tile'), may hold values from 0 to 110, as said below
Outputs:
- grad: float32 [128, 972, 1024], P('tile', 'dp', 'map')
- new_weights: bfloat16 [128, 972, 1024], P('tile', None, 'map')
The draws below stay inside these ranges and needn't reach their ends.
Inputs may be any that keep to these rules, and one draw needn't show every extreme that they name: offsets[c, 0] lies in 0 to 19 and offsets[c, 1] in 0 to 110; in every tile some column has both at their largest and some has both at zero.
All inputs are finite; a program needn't handle non-finite values.
Results may differ from the reference program's by a relative error of at most 0.017.
Values may be sent and summed in bfloat16 or wider, within the bound.
No kernel may reach another device: no remote copies, remote signals or barrier semaphores. Data moves between devices by JAX's collectives and lax.ppermute only.
A program may use at most 128 MiB of HBM per device.

```python
import jax
import jax.numpy as jnp
from jax import lax

FIELD = 18
CH = 3
MAPS = 1024
POOL = 5
ROWS_DEV = 20
WIDTH = 128
COLS_DEV = 8
IN = 972
MAPS_DEV = 128
COLS = 128
FRAMES = 768
HEIGHT = 320
N_MAP = 8


def draw_offsets(key, part):
    key = jax.random.fold_in(key, 11)
    first_key, second_key, third_key, fourth_key = jax.random.split(key, 4)
    tops = jax.random.randint(first_key, (COLS,), 0, ROWS_DEV)
    lefts = jax.random.randint(second_key, (COLS,), 0, WIDTH - FIELD + 1)
    tiles = COLS // COLS_DEV
    high_slot = jax.random.randint(third_key, (tiles,), 0, COLS_DEV)
    step_away = jax.random.randint(fourth_key, (tiles,), 1, COLS_DEV)
    low_slot = (high_slot + step_away) % COLS_DEV
    slot = jnp.arange(COLS) % COLS_DEV
    tile_of = jnp.arange(COLS) // COLS_DEV
    is_high = slot == high_slot[tile_of]
    is_low = slot == low_slot[tile_of]
    tops = jnp.where(is_high, ROWS_DEV - 1, jnp.where(is_low, 0, tops))
    lefts = jnp.where(is_high, WIDTH - FIELD, jnp.where(is_low, 0, lefts))
    return jnp.stack([tops, lefts], axis=1).astype(jnp.int32)


def shard_levels(own_key, dims, cuts, least, high):
    def one(position, parts):
        draws = jax.random.uniform(jax.random.fold_in(jax.random.fold_in(own_key, 6), position), (parts,), jnp.float32, least / len(cuts), high / len(cuts))
        return jnp.repeat(jnp.exp(draws), dims[position] // parts).reshape((-1,) + (1,) * (len(dims) - position - 1))

    gain = one(*cuts[0])
    for cut in cuts[1:]:
        gain = gain * one(*cut)
    return gain


def centred(stream_key, extent, scale, most, shards=(), held_as=jnp.bfloat16):
    drawn = scale * jax.random.normal(stream_key, extent, jnp.float32)
    if shards:
        drawn = drawn * shard_levels(stream_key, extent, shards, -0.22, 0.18)
    return jnp.clip(drawn, -most, most).astype(held_as)


def setup_inputs(seed: int = 0) -> dict:
    arg_keys = jax.random.split(jax.random.key(seed), 4)
    frames = centred(arg_keys[0], (CH, HEIGHT, WIDTH, FRAMES), 1.0, 6.0, ((1, 16), (3, 2)))
    weights = centred(arg_keys[1], (COLS, IN, MAPS), IN ** -0.5, 0.1875, ((0, 16), (2, 8)))
    offsets = draw_offsets(jax.random.fold_in(arg_keys[3], 71), 0)
    return {"frames": frames, "weights": weights, "offsets": offsets}


smoothing = 1.0
sparsity = 3.0
learn_rate = 0.1

def column_step(tall, weight, offset, column):
    tile_number = (column // COLS_DEV).astype(jnp.int32)
    top_row = (tile_number * ROWS_DEV + offset[0]).astype(jnp.int32)
    left_col = offset[1].astype(jnp.int32)
    zero = jnp.int32(0)
    patch = lax.dynamic_slice(tall, (zero, top_row, left_col, zero), (CH, FIELD, FIELD, FRAMES))
    pixels = patch.reshape(IN, FRAMES).T
    responses = jnp.dot(pixels, weight, preferred_element_type=jnp.float32)
    responses_b = responses.astype(jnp.bfloat16)
    rebuilt = jnp.zeros((FRAMES, IN), jnp.float32)
    for group in range(N_MAP):
        first = group * MAPS_DEV
        term = jnp.dot(responses_b[:, first:first + MAPS_DEV], weight[:, first:first + MAPS_DEV].T, preferred_element_type=jnp.float32).astype(jnp.bfloat16)
        rebuilt = rebuilt + lax.optimization_barrier(term).astype(jnp.float32)
    error_b = (rebuilt - pixels.astype(jnp.float32)).astype(jnp.bfloat16)
    back = jnp.dot(error_b, weight, preferred_element_type=jnp.float32)
    squares = responses * responses
    window = squares
    for shift_no in range(1, POOL):
        window = window + jnp.roll(squares, -shift_no, axis=1)
    inverse = 1.0 / jnp.sqrt(smoothing + window)
    spread = inverse
    for shift_no in range(1, POOL):
        spread = spread + jnp.roll(inverse, shift_no, axis=1)
    mixed = (back + sparsity * responses * spread).astype(jnp.bfloat16)
    grad = (jnp.dot(pixels.T, mixed, preferred_element_type=jnp.float32) + jnp.dot(error_b.T, responses_b, preferred_element_type=jnp.float32)) * (1.0 / FRAMES)
    fresh = (weight.astype(jnp.float32) - learn_rate * grad).astype(jnp.bfloat16)
    return (grad, fresh)

def reference(frames, weights, offsets):
    tall = jnp.pad(frames, ((0, 0), (0, FIELD - 1), (0, 0), (0, 0)))
    columns = jnp.arange(COLS, dtype=jnp.int32)

    def one(item):
        weight, offset, column = item
        return column_step(tall, weight, offset, column)
    grad, new_weights = lax.map(one, (weights, offsets, columns))
    return (grad, new_weights)
```

```python
import jax
import jax.numpy as jnp
from jax import lax
from jax.sharding import PartitionSpec as P

FIELD = 18
POOL = 5
CORES = 2

smoothing = 1.0
sparsity = 3.0
learn_rate = 0.1

AXES = ("tile", "map", "dp")


def table(mesh_shape, move):
    tiles, maps, dps = mesh_shape
    pairs = []
    for t in range(tiles):
        for y in range(maps // CORES):
            for k in range(CORES):
                for d in range(dps):
                    to = move(t, y, k, d)
                    if to is None:
                        continue
                    t2, y2, k2, d2 = to
                    if not 0 <= t2 < tiles:
                        continue
                    y2 = y2 % (maps // CORES)
                    source = (t * maps + y * CORES + k) * dps + d
                    target = (t2 * maps + y2 * CORES + k2) * dps + d2
                    pairs.append((source, target))
    return pairs


def cut(frames, place, above):
    channels, rows_here, wide, count = frames.shape
    zero = jnp.int32(0)
    strip = lax.dynamic_slice(
        frames, (zero, zero, place[1], zero), (channels, rows_here, FIELD, count)
    )
    if above:
        strip = jnp.pad(strip, ((0, 0), (0, FIELD - 1), (0, 0), (0, 0)))
    else:
        strip = jnp.pad(strip, ((0, 0), (rows_here, 0), (0, 0), (0, 0)))
    piece = lax.dynamic_slice(
        strip, (zero, place[0], zero, zero), (channels, FIELD, FIELD, count)
    )
    return piece.reshape(channels * FIELD * FIELD, count)


def ring_sum(x, step):
    total = x
    for shift in range(1, POOL):
        total = total + jnp.roll(x, step * shift, axis=1)
    return total


def column_step(patch, weight, total_frames):
    responses = jnp.einsum("if,im->fm", patch, weight, preferred_element_type=jnp.float32)
    responses_b = responses.astype(jnp.bfloat16)
    rebuilt = jnp.einsum("im,fm->if", weight, responses_b, preferred_element_type=jnp.float32)
    error_b = (rebuilt - patch.astype(jnp.float32)).astype(jnp.bfloat16)
    back = jnp.einsum("if,im->fm", error_b, weight, preferred_element_type=jnp.float32)
    inverse = 1.0 / jnp.sqrt(smoothing + ring_sum(responses * responses, -1))
    spread = ring_sum(inverse, 1)
    mixed = (back + sparsity * responses * spread).astype(jnp.bfloat16)
    return (
        jnp.einsum("if,fm->im", patch, mixed, preferred_element_type=jnp.float32)
        + jnp.einsum("if,fm->im", error_b, responses_b, preferred_element_type=jnp.float32)
    ) * (1.0 / total_frames)


def per_device(mesh_shape, frames, weights, offsets):
    num_cols, inner, maps_here = weights.shape
    rows_y = mesh_shape[1] // CORES
    group = lax.axis_index("map")
    y, k, d = group // CORES, group % CORES, lax.axis_index("dp")

    def send(x, move):
        return lax.ppermute(x, AXES, table(mesh_shape, move))

    upper_offsets = send(offsets, lambda t, y, k, d: (t + 1, y, k, d))
    lent = CORES * y + k
    below = cut(frames, upper_offsets[lent], False)
    above = cut(frames, offsets[lent], True)
    below = send(below, lambda t, y, k, d: (t - 1, y, d, k))
    above_in = send(above, lambda t, y, k, d: (t, y, d, k) if k != d else None)
    patch = jnp.where(k == d, above, above_in) + below

    own = []
    for s in range(rows_y):
        target = (y - s) % rows_y
        block = lax.dynamic_index_in_dim(weights, CORES * target + d, 0, keepdims=False)
        if s:
            block = send(block, lambda t, y, k, d: (t, y - s, k, d))
        own.append(block)
    own = jnp.stack(own, 1)
    other = send(own, lambda t, y, k, d: (t, y, 1 - k, d))
    low, high = jnp.where(k == 0, own, other), jnp.where(k == 0, other, own)
    weight = jnp.stack([low, high], 2).reshape(inner, -1)

    grad = column_step(patch, weight, frames.shape[3] * CORES)

    grad = grad.reshape(inner, rows_y, CORES, maps_here)
    low, high = grad[:, :, 0], grad[:, :, 1]
    away = jnp.where(k == 0, high, low).astype(jnp.bfloat16)
    home = jnp.where(k == 0, low, high)
    both = home + send(away, lambda t, y, k, d: (t, y, 1 - k, d)).astype(jnp.float32)
    both = both.astype(jnp.bfloat16)
    arrived = []
    for s in range(rows_y):
        block = both[:, s]
        if s:
            block = send(block, lambda t, y, k, d: (t, y + s, k, d))
        arrived.append(block)
    arrived = jnp.stack(arrived)
    crossed = send(arrived, lambda t, y, k, d: (t, y, k, 1 - d))
    order = (y - jnp.arange(rows_y)) % rows_y
    arrived, crossed = arrived[order], crossed[order]
    low, high = jnp.where(d == 0, arrived, crossed), jnp.where(d == 0, crossed, arrived)
    full = jnp.stack([low, high], 1).reshape(num_cols, inner, maps_here).astype(jnp.float32)
    half = inner // mesh_shape[2]
    new_weights = (weights.astype(jnp.float32) - learn_rate * full).astype(jnp.bfloat16)
    return lax.dynamic_slice_in_dim(full, d * half, half, 1), new_weights


def solution(mesh):
    mesh_shape = tuple(mesh.shape[a] for a in AXES)
    placed = (P(None, "tile", None, "dp"), P("tile", None, "map"), P("tile", None))

    def run(frames, weights, offsets):
        return per_device(mesh_shape, frames, weights, offsets)

    return jax.shard_map(
        run,
        mesh=mesh,
        in_specs=placed,
        out_specs=(P("tile", "dp", "map"), P("tile", None, "map")),
        check_vma=False,
    )
```

```python
import functools

import jax
import jax.numpy as jnp
from jax import lax
from jax.experimental import pallas as pl
from jax.experimental.pallas import tpu as pltpu
from jax.sharding import PartitionSpec as P

FIELD = 18
POOL = 5
CORES = 2
STRIP = 48
SUB = 8
LANES = 128
MIB = 1 << 20

smoothing = 1.0
sparsity = 3.0
learn_rate = 0.1

AXES = ("tile", "map", "dp")
F32, BF16 = jnp.float32, jnp.bfloat16
VMEM = pl.BlockSpec(memory_space=pltpu.VMEM)
SMEM = pl.BlockSpec(memory_space=pltpu.SMEM)
ANY = pl.BlockSpec(memory_space=pl.ANY)
HBM = pl.BlockSpec(memory_space=pltpu.HBM)


def table(mesh_shape, move):
    tiles, maps, dps = mesh_shape
    rows_y = maps // CORES
    pairs = []
    for t in range(tiles):
        for y in range(rows_y):
            for k in range(CORES):
                for d in range(dps):
                    to = move(t, y, k, d)
                    if to is None or not 0 <= to[0] < tiles:
                        continue
                    t2, y2, k2, d2 = to
                    source = (t * maps + y * CORES + k) * dps + d
                    target = (t2 * maps + (y2 % rows_y) * CORES + k2) * dps + d2
                    pairs.append((source, target))
    return pairs


def params(mib):
    return pltpu.CompilerParams(vmem_limit_bytes=mib * MIB)


def cut_kernel(above, offsets, frames, *refs):
    out, strip, flat, sem = refs[-4:]
    channels, rows_here, wide, count = frames.shape
    column = lax.axis_index("map")
    top, left = offsets[column, 0], offsets[column, 1]
    base = jnp.minimum(left // 16 * 16, wide - STRIP)
    base = pl.multiple_of(base, 16)
    first = jnp.minimum(top, rows_here - FIELD) if above else 0
    copy = pltpu.make_async_copy(
        frames.at[:, pl.ds(first, FIELD), pl.ds(base, STRIP), :], strip, sem
    )
    copy.start()
    copy.wait()
    back = lax.rem(STRIP - (left - base), STRIP)
    for channel in range(channels):
        for r in range(FIELD):
            row = top + r - (first if above else rows_here)
            valid = (row < FIELD) if above else (row >= 0)
            row = jnp.clip(row, 0, FIELD - 1)
            x = strip[channel, row].astype(F32)
            x = pltpu.roll(x, back, 0)[: FIELD + 6]
            x = jnp.where(valid, x, 0.0)
            flat[pl.ds((channel * FIELD + r) * FIELD, FIELD + 6), :] = x
    inner = channels * FIELD * FIELD
    out[...] = flat[pl.ds(0, inner), :].astype(BF16)


def cut(frames, offsets, above, after=()):
    channels, rows_here, wide, count = frames.shape
    inner = channels * FIELD * FIELD
    return pl.pallas_call(
        functools.partial(cut_kernel, above),
        out_shape=jax.ShapeDtypeStruct((inner, count), BF16),
        in_specs=[SMEM, HBM] + [ANY] * len(after),
        out_specs=VMEM,
        scratch_shapes=[
            pltpu.VMEM((channels, FIELD, STRIP, count), BF16),
            pltpu.VMEM((inner + 12, count), F32),
            pltpu.SemaphoreType.DMA,
        ],
        compiler_params=params(16 if above else 58),
        name="cut_above" if above else "cut_below",
    )(offsets, frames, *after)


def blocks_kernel(rows_y, dps, flat, after, *refs):
    outs, wide = refs[:-1], refs[-1]
    inner = outs[0].shape[0]
    y, d = lax.axis_index("map") // CORES, lax.axis_index("dp")
    wide[...] = flat[...].astype(F32)
    for s in range(rows_y):
        column = dps * lax.rem(y + rows_y - s, rows_y) + d
        outs[s][...] = wide[pl.ds(column, inner, stride=rows_y * dps), :].astype(BF16)


def blocks(weights, rows_y, dps, after):
    num_cols, inner, here = weights.shape
    flat = weights.transpose(1, 0, 2).reshape(inner * num_cols, here)
    return pl.pallas_call(
        functools.partial(blocks_kernel, rows_y, dps),
        out_shape=[jax.ShapeDtypeStruct((inner, here), BF16)] * rows_y,
        in_specs=[VMEM, ANY],
        out_specs=[VMEM] * rows_y,
        scratch_shapes=[pltpu.VMEM(flat.shape, F32)],
        compiler_params=params(16),
        name="blocks",
    )(flat, after)


def filters_kernel(own, other, weight, turned):
    k = lax.rem(lax.axis_index("map"), CORES)
    for block, core in ((own[...], k), (other[...], 1 - k)):
        at = pl.multiple_of(core * LANES, LANES)
        weight[:, pl.ds(at, LANES)] = block
        turned[pl.ds(at, LANES), :] = block.T


def filters(own, other):
    inner, here = own.shape
    return pl.pallas_call(
        filters_kernel,
        out_shape=[
            jax.ShapeDtypeStruct((inner, CORES * here), BF16),
            jax.ShapeDtypeStruct((CORES * here, inner), BF16),
        ],
        in_specs=[VMEM] * 2,
        out_specs=[VMEM] * 2,
        compiler_params=params(8),
        name="filters",
    )(own, other)


def dot(a, b):
    return jnp.dot(a, b, preferred_element_type=F32)


def column_kernel(rows_y, above, above_in, below, *refs):
    weight, turned = refs[:rows_y], refs[rows_y : 2 * rows_y]
    pe, mr, res, sq, inv = refs[2 * rows_y :]
    inner, count = above.shape
    tile = weight[0].shape[1]
    maps = rows_y * tile
    mine = lax.rem(lax.axis_index("map"), CORES) == lax.axis_index("dp")

    @pl.when(mine)
    def _():
        pe[:, pl.ds(0, count)] = above[...] + below[...]

    @pl.when(jnp.logical_not(mine))
    def _():
        pe[:, pl.ds(0, count)] = above_in[...] + below[...]

    patch = pe[:, pl.ds(0, count)]
    for m in range(0, maps, tile):
        r = dot(turned[m // tile][...], patch)
        res[pl.ds(m, tile), :] = r
        mr[pl.ds(m, tile), pl.ds(count, count)] = r.astype(BF16)
        sq[pl.ds(m, tile), :] = r * r
    sq[pl.ds(maps, SUB), :] = sq[pl.ds(0, SUB), :]

    steps = -(-inner // tile)
    for n in range(steps):
        low, high = n * tile, min(inner, (n + 1) * tile)
        rows = pl.ds(low, high - low)
        error = -pe[rows, pl.ds(0, count)].astype(F32)
        for p in range(rows_y):
            error += dot(weight[p][rows, :], mr[pl.ds(p * tile, tile), pl.ds(count, count)])
        pe[rows, pl.ds(count, count)] = error.astype(BF16)
    for m in range(0, maps, tile):
        total = sq[pl.ds(m, tile), :]
        for i in range(1, POOL):
            total = total + sq[pl.ds(m + i, tile), :]
        inv[pl.ds(SUB + m, tile), :] = lax.rsqrt(smoothing + total)
    inv[pl.ds(0, SUB), :] = inv[pl.ds(maps, SUB), :]
    error_b = pe[:, pl.ds(count, count)]
    for m in range(0, maps, tile):
        back = dot(turned[m // tile][...], error_b)
        spread = inv[pl.ds(SUB + m, tile), :]
        for i in range(1, POOL):
            spread = spread + inv[pl.ds(SUB + m - i, tile), :]
        mixed = back + sparsity * res[pl.ds(m, tile), :] * spread
        mr[pl.ds(m, tile), pl.ds(0, count)] = mixed.astype(BF16)


def column(above, above_in, below, weight, turned):
    inner, count = above.shape
    rows_y = len(weight)
    maps = rows_y * weight[0].shape[1]
    return pl.pallas_call(
        functools.partial(column_kernel, rows_y),
        out_shape=[
            jax.ShapeDtypeStruct((inner, 2 * count), BF16),
            jax.ShapeDtypeStruct((maps, 2 * count), BF16),
        ],
        in_specs=[VMEM] * (3 + 2 * rows_y),
        out_specs=[VMEM] * 2,
        scratch_shapes=[
            pltpu.VMEM((maps, count), F32),
            pltpu.VMEM((maps + SUB, count), F32),
            pltpu.VMEM((maps + SUB, count), F32),
        ],
        compiler_params=params(40),
        name="column",
    )(above, above_in, below, *weight, *turned)


def piece_kernel(p, scale, pe, mr, home, away):
    inner = pe.shape[0]
    first = lax.rem(lax.axis_index("map"), CORES) == 0
    tile = 256
    groups = mr[pl.ds(CORES * LANES * p, CORES * LANES), :]
    for n in range(0, inner, tile):
        rows = pl.ds(n, min(tile, inner - n))
        g = lax.dot_general(
            pe[rows, :], groups, (((1,), (1,)), ((), ())), preferred_element_type=F32
        )
        g = g * scale
        low, high = g[:, :LANES], g[:, LANES:]
        home[rows, :] = jnp.where(first, low, high)
        away[rows, :] = jnp.where(first, high, low).astype(BF16)


def piece(p, pe, mr):
    inner, depth = pe.shape
    return pl.pallas_call(
        functools.partial(piece_kernel, p, 1.0 / depth),
        out_shape=[
            jax.ShapeDtypeStruct((inner, LANES), F32),
            jax.ShapeDtypeStruct((inner, LANES), BF16),
        ],
        in_specs=[VMEM] * 2,
        out_specs=[VMEM] * 2,
        compiler_params=params(16),
        name="piece",
    )(pe, mr)


def finish_kernel(rows_y, dps, *refs):
    arrived, crossed = refs[:rows_y], refs[rows_y : 2 * rows_y]
    weights, grad, fresh, full = refs[2 * rows_y :]
    inner = arrived[0].shape[0]
    num_cols = rows_y * dps
    y, d = lax.axis_index("map") // CORES, lax.axis_index("dp")
    for s in range(rows_y):
        row = lax.rem(y + rows_y - s, rows_y)
        for block, part in ((arrived[s], d), (crossed[s], 1 - d)):
            full[pl.ds(dps * row + part, inner, stride=num_cols), :] = block[...].astype(F32)
    some = inner * num_cols // dps
    grad[...] = full[pl.ds(pl.multiple_of(d * some, SUB), some), :]
    fresh[...] = (weights[...].astype(F32) - learn_rate * full[...]).astype(BF16)


def finish(arrived, crossed, weights, dps):
    inner, here = arrived[0].shape
    num_cols = weights.shape[0]
    rows = inner * num_cols
    flat = weights.transpose(1, 0, 2).reshape(rows, here)
    grad, fresh = pl.pallas_call(
        functools.partial(finish_kernel, len(arrived), dps),
        out_shape=[
            jax.ShapeDtypeStruct((rows // dps, here), F32),
            jax.ShapeDtypeStruct((rows, here), BF16),
        ],
        in_specs=[VMEM] * (2 * len(arrived) + 1),
        out_specs=[VMEM] * 2,
        scratch_shapes=[pltpu.VMEM((rows, here), F32)],
        compiler_params=params(32),
        name="finish",
    )(*arrived, *crossed, flat)
    grad = grad.reshape(inner // dps, num_cols, here).transpose(1, 0, 2)
    return grad, fresh.reshape(inner, num_cols, here).transpose(1, 0, 2)


def per_device(mesh_shape, frames, weights, offsets):
    rows_y = mesh_shape[1] // CORES
    def send(x, move):
        return lax.ppermute(x, AXES, table(mesh_shape, move))

    upper_offsets = send(offsets, lambda t, y, k, d: (t + 1, y, k, d))
    below = cut(frames, upper_offsets, False)
    own = blocks(weights, rows_y, mesh_shape[2], below)
    above = cut(frames, offsets, True, own[:1])
    below = send(below, lambda t, y, k, d: (t - 1, y, d, k))
    above_in = send(above, lambda t, y, k, d: (t, y, d, k) if k != d else None)

    weight, turned = [], []
    for s in range(rows_y):
        block = own[s]
        if s:
            block = send(block, lambda t, y, k, d: (t, y - s, k, d))
        other = send(block, lambda t, y, k, d: (t, y, 1 - k, d))
        pair = filters(block, other)
        weight.append(pair[0])
        turned.append(pair[1])

    pe, mr = column(above, above_in, below, weight, turned)

    arrived, crossed = [], []
    for s in range(rows_y):
        home, away = piece(s, pe, mr)
        away = send(away, lambda t, y, k, d: (t, y, 1 - k, d))
        block = (home + away.astype(F32)).astype(BF16)
        if s:
            block = send(block, lambda t, y, k, d: (t, y + s, k, d))
        arrived.append(block)
        crossed.append(send(block, lambda t, y, k, d: (t, y, k, 1 - d)))
    return finish(arrived, crossed, weights, mesh_shape[2])


def solution(mesh):
    mesh_shape = tuple(mesh.shape[a] for a in AXES)
    placed = (P(None, "tile", None, "dp"), P("tile", None, "map"), P("tile", None))

    def run(frames, weights, offsets):
        return per_device(mesh_shape, frames, weights, offsets)

    return jax.shard_map(
        run,
        mesh=mesh,
        in_specs=placed,
        out_specs=(P("tile", "dp", "map"), P("tile", None, "map")),
        check_vma=False,
    )
```

```python
import functools

import jax
import jax.numpy as jnp
from jax import lax
from jax.experimental import pallas as pl
from jax.experimental.pallas import tpu as pltpu
from jax.sharding import PartitionSpec as P

FIELD = 18
POOL = 5
CORES = 2
STRIP = 48
SUB = 8
LANES = 128
MIB = 1 << 20
CUT_MIB = 50
OUT_ROWS = 2048

smoothing = 1.0
sparsity = 3.0
learn_rate = 0.1

AXES = ("tile", "map", "dp")
F32, BF16 = jnp.float32, jnp.bfloat16
VMEM = pl.BlockSpec(memory_space=pltpu.VMEM)
SMEM = pl.BlockSpec(memory_space=pltpu.SMEM)
ANY = pl.BlockSpec(memory_space=pl.ANY)
HBM = pl.BlockSpec(memory_space=pltpu.HBM)


def table(mesh_shape, move):
    tiles, maps, dps = mesh_shape
    rows_y = maps // CORES
    pairs = []
    for t in range(tiles):
        for y in range(rows_y):
            for k in range(CORES):
                for d in range(dps):
                    to = move(t, y, k, d)
                    if to is None or not 0 <= to[0] < tiles:
                        continue
                    t2, y2, k2, d2 = to
                    source = (t * maps + y * CORES + k) * dps + d
                    target = (t2 * maps + (y2 % rows_y) * CORES + k2) * dps + d2
                    pairs.append((source, target))
    return pairs


def params(mib):
    return pltpu.CompilerParams(vmem_limit_bytes=mib * MIB)


def cut_kernel(above, places, frames, *refs):
    out, token, strip, flat, sems = refs[-5:]
    channels, rows_here, wide, count = frames.shape
    column = lax.axis_index("map")
    top, left = places[0, column], places[1, column]
    base = jnp.minimum(left // 16 * 16, wide - STRIP)
    base = pl.multiple_of(base, 16)
    first = jnp.minimum(top, rows_here - FIELD) if above else 0
    copies = [
        pltpu.make_async_copy(
            frames.at[channel, pl.ds(first, FIELD), pl.ds(base, STRIP), :],
            strip.at[channel],
            sems.at[channel],
        )
        for channel in range(channels)
    ]
    for copy in copies:
        copy.start()
    token[...] = jnp.zeros_like(token)
    back = lax.rem(STRIP - (left - base), STRIP)
    for channel in range(channels):
        copies[channel].wait()
        for r in range(FIELD):
            row = top + r - (first if above else rows_here)
            valid = (row < FIELD) if above else (row >= 0)
            row = jnp.clip(row, 0, FIELD - 1)
            x = strip[channel, row].astype(F32)
            x = pltpu.roll(x, back, 0)[: FIELD + 6]
            x = jnp.where(valid, x, 0.0)
            flat[pl.ds((channel * FIELD + r) * FIELD, FIELD + 6), :] = x
    inner = channels * FIELD * FIELD
    out[...] = flat[pl.ds(0, inner), :].astype(BF16)


def cut(frames, places, above, after=()):
    channels, rows_here, wide, count = frames.shape
    inner = channels * FIELD * FIELD
    return pl.pallas_call(
        functools.partial(cut_kernel, above),
        out_shape=[
            jax.ShapeDtypeStruct((inner, count), BF16),
            jax.ShapeDtypeStruct((SUB, LANES), F32),
        ],
        in_specs=[SMEM, HBM] + [ANY] * len(after),
        out_specs=[VMEM] * 2,
        scratch_shapes=[
            pltpu.VMEM((channels, FIELD, STRIP, count), BF16),
            pltpu.VMEM((inner + 12, count), F32),
            pltpu.SemaphoreType.DMA((channels,)),
        ],
        compiler_params=params(CUT_MIB),
        name="cut_above" if above else "cut_below",
    )(places, frames, *after)


def blocks_kernel(rows_y, dps, flat, *refs):
    outs, wide = refs[-1 - rows_y : -1], refs[-1]
    inner = outs[0].shape[0]
    y, d = lax.axis_index("map") // CORES, lax.axis_index("dp")
    wide[...] = flat[...].astype(F32)
    for s in range(rows_y):
        column = dps * lax.rem(y + rows_y - s, rows_y) + d
        outs[s][...] = wide[pl.ds(column, inner, stride=rows_y * dps), :].astype(BF16)


def blocks(weights, rows_y, dps, after=()):
    num_cols, inner, here = weights.shape
    flat = weights.transpose(1, 0, 2).reshape(inner * num_cols, here)
    return pl.pallas_call(
        functools.partial(blocks_kernel, rows_y, dps),
        out_shape=[jax.ShapeDtypeStruct((inner, here), BF16)] * rows_y,
        in_specs=[VMEM] + [ANY] * len(after),
        out_specs=[VMEM] * rows_y,
        scratch_shapes=[pltpu.VMEM(flat.shape, F32)],
        compiler_params=params(16),
        name="blocks",
    )(flat, *after)


def filters_kernel(own, other, weight, turned):
    k = lax.rem(lax.axis_index("map"), CORES)
    for block, core in ((own[...], k), (other[...], 1 - k)):
        at = pl.multiple_of(core * LANES, LANES)
        weight[:, pl.ds(at, LANES)] = block
        turned[pl.ds(at, LANES), :] = block.T


def filters(own, other):
    inner, here = own.shape
    return pl.pallas_call(
        filters_kernel,
        out_shape=[
            jax.ShapeDtypeStruct((inner, CORES * here), BF16),
            jax.ShapeDtypeStruct((CORES * here, inner), BF16),
        ],
        in_specs=[VMEM] * 2,
        out_specs=[VMEM] * 2,
        compiler_params=params(8),
        name="filters",
    )(own, other)


def dot(a, b):
    return jnp.dot(a, b, preferred_element_type=F32)


def column_kernel(rows_y, above, above_in, below, *refs):
    weight, turned = refs[:rows_y], refs[rows_y : 2 * rows_y]
    pe, mr, res, sq, inv = refs[2 * rows_y :]
    inner, count = above.shape
    tile = weight[0].shape[1]
    maps = rows_y * tile
    mine = lax.rem(lax.axis_index("map"), CORES) == lax.axis_index("dp")

    @pl.when(mine)
    def _():
        pe[:, pl.ds(0, count)] = above[...] + below[...]

    @pl.when(jnp.logical_not(mine))
    def _():
        pe[:, pl.ds(0, count)] = above_in[...] + below[...]

    patch = pe[:, pl.ds(0, count)]
    for m in range(0, maps, tile):
        r = dot(turned[m // tile][...], patch)
        res[pl.ds(m, tile), :] = r
        mr[pl.ds(m, tile), pl.ds(count, count)] = r.astype(BF16)
        sq[pl.ds(m, tile), :] = r * r
    sq[pl.ds(maps, SUB), :] = sq[pl.ds(0, SUB), :]

    steps = -(-inner // tile)
    for n in range(steps):
        low, high = n * tile, min(inner, (n + 1) * tile)
        rows = pl.ds(low, high - low)
        error = -pe[rows, pl.ds(0, count)].astype(F32)
        for p in range(rows_y):
            error += dot(weight[p][rows, :], mr[pl.ds(p * tile, tile), pl.ds(count, count)])
        pe[rows, pl.ds(count, count)] = error.astype(BF16)
    for m in range(0, maps, tile):
        total = sq[pl.ds(m, tile), :]
        for i in range(1, POOL):
            total = total + sq[pl.ds(m + i, tile), :]
        inv[pl.ds(SUB + m, tile), :] = lax.rsqrt(smoothing + total)
    inv[pl.ds(0, SUB), :] = inv[pl.ds(maps, SUB), :]
    error_b = pe[:, pl.ds(count, count)]
    for m in range(0, maps, tile):
        back = dot(turned[m // tile][...], error_b)
        spread = inv[pl.ds(SUB + m, tile), :]
        for i in range(1, POOL):
            spread = spread + inv[pl.ds(SUB + m - i, tile), :]
        mixed = back + sparsity * res[pl.ds(m, tile), :] * spread
        mr[pl.ds(m, tile), pl.ds(0, count)] = mixed.astype(BF16)


def column(above, above_in, below, weight, turned):
    inner, count = above.shape
    rows_y = len(weight)
    maps = rows_y * weight[0].shape[1]
    return pl.pallas_call(
        functools.partial(column_kernel, rows_y),
        out_shape=[
            jax.ShapeDtypeStruct((inner, 2 * count), BF16),
            jax.ShapeDtypeStruct((maps, 2 * count), BF16),
        ],
        in_specs=[VMEM] * (3 + 2 * rows_y),
        out_specs=[VMEM] * 2,
        scratch_shapes=[
            pltpu.VMEM((maps, count), F32),
            pltpu.VMEM((maps + SUB, count), F32),
            pltpu.VMEM((maps + SUB, count), F32),
        ],
        compiler_params=params(40),
        name="column",
    )(above, above_in, below, *weight, *turned)


def piece_kernel(p, scale, pe, mr, home, away):
    inner = pe.shape[0]
    first = lax.rem(lax.axis_index("map"), CORES) == 0
    tile = 256
    groups = mr[pl.ds(CORES * LANES * p, CORES * LANES), :]
    for n in range(0, inner, tile):
        rows = pl.ds(n, min(tile, inner - n))
        g = lax.dot_general(
            pe[rows, :], groups, (((1,), (1,)), ((), ())), preferred_element_type=F32
        )
        g = g * scale
        low, high = g[:, :LANES], g[:, LANES:]
        home[rows, :] = jnp.where(first, low, high)
        away[rows, :] = jnp.where(first, high, low).astype(BF16)


def piece(p, pe, mr):
    inner, depth = pe.shape
    return pl.pallas_call(
        functools.partial(piece_kernel, p, 1.0 / depth),
        out_shape=[
            jax.ShapeDtypeStruct((inner, LANES), F32),
            jax.ShapeDtypeStruct((inner, LANES), BF16),
        ],
        in_specs=[VMEM] * 2,
        out_specs=[VMEM] * 2,
        compiler_params=params(16),
        name="piece",
    )(pe, mr)


def place_pieces(full, shifts, refs, rows_y, dps):
    y, d = lax.axis_index("map") // CORES, lax.axis_index("dp")
    inner = refs[0].shape[0]
    for n, s in enumerate(shifts):
        row = lax.rem(y + rows_y - s, rows_y)
        for block, part in ((refs[2 * n], d), (refs[2 * n + 1], 1 - d)):
            at = pl.ds(dps * row + part, inner, stride=rows_y * dps)
            full[at, :] = block[...].astype(F32)


def gather_kernel(rows_y, dps, shifts, *refs):
    place_pieces(refs[-1], shifts, refs[:-1], rows_y, dps)


def gather(pieces, shifts, rows_y, dps):
    inner, here = pieces[0].shape
    return pl.pallas_call(
        functools.partial(gather_kernel, rows_y, dps, shifts),
        out_shape=jax.ShapeDtypeStruct((inner * rows_y * dps, here), F32),
        in_specs=[VMEM] * len(pieces),
        out_specs=VMEM,
        compiler_params=params(8),
        name="gather",
    )(*pieces)


def finish_kernel(rows_y, dps, shifts, *refs):
    pieces, weights, early = refs[: 2 * len(shifts)], refs[-8], refs[-7]
    grad, fresh, full, new, grad_sem, sems = refs[-6:]
    full[...] = early[...]
    place_pieces(full, shifts, pieces, rows_y, dps)
    rows = full.shape[0]
    some = rows // dps
    at = pl.multiple_of(lax.axis_index("dp") * some, SUB)
    grad_copy = pltpu.make_async_copy(full.at[pl.ds(at, some), :], grad, grad_sem)
    grad_copy.start()
    copies = []
    for n, low in enumerate(range(0, rows, OUT_ROWS)):
        part = pl.ds(low, min(OUT_ROWS, rows - low))
        new[part, :] = (weights[part, :].astype(F32) - learn_rate * full[part, :]).astype(BF16)
        copy = pltpu.make_async_copy(new.at[part, :], fresh.at[part, :], sems.at[n])
        copy.start()
        copies.append(copy)
    grad_copy.wait()
    for copy in copies:
        copy.wait()


def finish(pieces, shifts, weights, full, rows_y, dps):
    num_cols, inner, here = weights.shape
    rows = inner * num_cols
    flat = weights.transpose(1, 0, 2).reshape(rows, here)
    grad, fresh = pl.pallas_call(
        functools.partial(finish_kernel, rows_y, dps, shifts),
        out_shape=[
            jax.ShapeDtypeStruct((rows // dps, here), F32),
            jax.ShapeDtypeStruct((rows, here), BF16),
        ],
        in_specs=[VMEM] * (len(pieces) + 2),
        out_specs=[HBM, HBM],
        scratch_shapes=[
            pltpu.VMEM((rows, here), F32),
            pltpu.VMEM((rows, here), BF16),
            pltpu.SemaphoreType.DMA,
            pltpu.SemaphoreType.DMA((-(-rows // OUT_ROWS),)),
        ],
        compiler_params=params(16),
        name="finish",
    )(*pieces, flat, full)
    grad = grad.reshape(inner // dps, num_cols, here).transpose(1, 0, 2)
    return grad, fresh.reshape(inner, num_cols, here).transpose(1, 0, 2)


def per_device(mesh_shape, frames, weights, offsets):
    rows_y = mesh_shape[1] // CORES
    def send(x, move):
        return lax.ppermute(x, AXES, table(mesh_shape, move))

    dps = mesh_shape[2]
    places = offsets.T
    upper = send(places, lambda t, y, k, d: (t + 1, y, k, d))
    below, token = cut(frames, upper, False)
    own = blocks(weights, rows_y, dps, (token,))
    above, token = cut(frames, places, True, (own[0],))
    below = send(below, lambda t, y, k, d: (t - 1, y, d, k))
    above_in = send(above, lambda t, y, k, d: (t, y, d, k) if k != d else None)

    weight, turned = [], []
    for s in range(rows_y):
        block = own[s]
        if s:
            block = send(block, lambda t, y, k, d: (t, y - s, k, d))
        other = send(block, lambda t, y, k, d: (t, y, 1 - k, d))
        pair = filters(block, other)
        weight.append(pair[0])
        turned.append(pair[1])

    pe, mr = column(above, above_in, below, weight, turned)

    pieces = {}
    for s in (1, 0, 3, 2):
        home, away = piece(s, pe, mr)
        away = send(away, lambda t, y, k, d: (t, y, 1 - k, d))
        block = (home + away.astype(F32)).astype(BF16)
        if s:
            block = send(block, lambda t, y, k, d: (t, y + s, k, d))
        pieces[s] = [block, send(block, lambda t, y, k, d: (t, y, k, 1 - d))]
    early, late = (0, 1, 3), (2,)
    full = gather(sum([pieces[s] for s in early], []), early, rows_y, dps)
    return finish(sum([pieces[s] for s in late], []), late, weights, full, rows_y, dps)


def solution(mesh):
    mesh_shape = tuple(mesh.shape[a] for a in AXES)
    placed = (P(None, "tile", None, "dp"), P("tile", None, "map"), P("tile", None))

    def run(frames, weights, offsets):
        return per_device(mesh_shape, frames, weights, offsets)

    return jax.shard_map(
        run,
        mesh=mesh,
        in_specs=placed,
        out_specs=(P("tile", "dp", "map"), P("tile", None, "map")),
        check_vma=False,
    )
```

```python
import functools

import jax
import jax.numpy as jnp
from jax import lax
from jax.experimental import pallas as pl
from jax.experimental.pallas import tpu as pltpu
from jax.sharding import PartitionSpec as P

FIELD = 18
POOL = 5
CORES = 2
STRIP = 48
SUB = 8
LANES = 128
MIB = 1 << 20
CUT_MIB = 50
OUT_ROWS = 2048

smoothing = 1.0
sparsity = 3.0
learn_rate = 0.1

AXES = ("tile", "map", "dp")
F32, BF16 = jnp.float32, jnp.bfloat16
VMEM = pl.BlockSpec(memory_space=pltpu.VMEM)
SMEM = pl.BlockSpec(memory_space=pltpu.SMEM)
ANY = pl.BlockSpec(memory_space=pl.ANY)
HBM = pl.BlockSpec(memory_space=pltpu.HBM)


def table(mesh_shape, move):
    tiles, maps, dps = mesh_shape
    rows_y = maps // CORES
    pairs = []
    for t in range(tiles):
        for y in range(rows_y):
            for k in range(CORES):
                for d in range(dps):
                    to = move(t, y, k, d)
                    if to is None or not 0 <= to[0] < tiles:
                        continue
                    t2, y2, k2, d2 = to
                    source = (t * maps + y * CORES + k) * dps + d
                    target = (t2 * maps + (y2 % rows_y) * CORES + k2) * dps + d2
                    pairs.append((source, target))
    return pairs


def params(mib):
    return pltpu.CompilerParams(vmem_limit_bytes=mib * MIB)


def cut_kernel(above, places, frames, *refs):
    out, token, strip, wide, flat, sems = refs[-6:]
    channels, rows_here, across, count = frames.shape
    column = lax.axis_index("map")
    top, left = places[0, column], places[1, column]
    base = jnp.minimum(left // 16 * 16, across - STRIP)
    base = pl.multiple_of(base, 16)
    first = jnp.minimum(top, rows_here - FIELD) if above else 0
    copies = [
        pltpu.make_async_copy(
            frames.at[channel, pl.ds(first, FIELD), pl.ds(base, STRIP), :],
            strip.at[channel],
            sems.at[channel],
        )
        for channel in range(channels)
    ]
    for copy in copies:
        copy.start()
    token[...] = jnp.zeros_like(token)
    shift = left - base
    for channel in range(channels):
        copies[channel].wait()
        for n in range(count // LANES):
            lanes = strip[channel, :, :, pl.ds(n * LANES, LANES)]
            wide[n] = lanes.reshape(FIELD * STRIP, LANES).astype(F32)
        for r in range(FIELD):
            row = top + r - (first if above else rows_here)
            valid = (row < FIELD) if above else (row >= 0)
            row = jnp.clip(row, 0, FIELD - 1)
            for n in range(count // LANES):
                x = wide[n, pl.ds(row * STRIP + shift, FIELD), :]
                x = jnp.where(valid, x, 0.0)
                at = pl.ds((channel * FIELD + r) * FIELD, FIELD)
                flat[at, pl.ds(n * LANES, LANES)] = x
    inner = channels * FIELD * FIELD
    out[...] = flat[pl.ds(0, inner), :].astype(BF16)


def cut(frames, places, above, after=()):
    channels, rows_here, wide, count = frames.shape
    inner = channels * FIELD * FIELD
    return pl.pallas_call(
        functools.partial(cut_kernel, above),
        out_shape=[
            jax.ShapeDtypeStruct((inner, count), BF16),
            jax.ShapeDtypeStruct((SUB, LANES), F32),
        ],
        in_specs=[SMEM, HBM] + [ANY] * len(after),
        out_specs=[VMEM] * 2,
        scratch_shapes=[
            pltpu.VMEM((channels, FIELD, STRIP, count), BF16),
            pltpu.VMEM((count // LANES, FIELD * STRIP, LANES), F32),
            pltpu.VMEM((inner, count), F32),
            pltpu.SemaphoreType.DMA((channels,)),
        ],
        compiler_params=params(CUT_MIB),
        name="cut_above" if above else "cut_below",
    )(places, frames, *after)


def blocks_kernel(rows_y, dps, flat, *refs):
    outs, wide = refs[-1 - rows_y : -1], refs[-1]
    inner = outs[0].shape[0]
    y, d = lax.axis_index("map") // CORES, lax.axis_index("dp")
    wide[...] = flat[...].astype(F32)
    for s in range(rows_y):
        column = dps * lax.rem(y + rows_y - s, rows_y) + d
        outs[s][...] = wide[pl.ds(column, inner, stride=rows_y * dps), :].astype(BF16)


def blocks(weights, rows_y, dps, after=()):
    num_cols, inner, here = weights.shape
    flat = weights.transpose(1, 0, 2).reshape(inner * num_cols, here)
    return pl.pallas_call(
        functools.partial(blocks_kernel, rows_y, dps),
        out_shape=[jax.ShapeDtypeStruct((inner, here), BF16)] * rows_y,
        in_specs=[VMEM] + [ANY] * len(after),
        out_specs=[VMEM] * rows_y,
        scratch_shapes=[pltpu.VMEM(flat.shape, F32)],
        compiler_params=params(16),
        name="blocks",
    )(flat, *after)


def filters_kernel(own, other, weight, turned):
    k = lax.rem(lax.axis_index("map"), CORES)
    for block, core in ((own[...], k), (other[...], 1 - k)):
        at = pl.multiple_of(core * LANES, LANES)
        weight[:, pl.ds(at, LANES)] = block
        turned[pl.ds(at, LANES), :] = block.T


def filters(own, other):
    inner, here = own.shape
    return pl.pallas_call(
        filters_kernel,
        out_shape=[
            jax.ShapeDtypeStruct((inner, CORES * here), BF16),
            jax.ShapeDtypeStruct((CORES * here, inner), BF16),
        ],
        in_specs=[VMEM] * 2,
        out_specs=[VMEM] * 2,
        compiler_params=params(8),
        name="filters",
    )(own, other)


def join_kernel(above, above_in, below, patch):
    mine = lax.rem(lax.axis_index("map"), CORES) == lax.axis_index("dp")

    @pl.when(mine)
    def _():
        patch[...] = above[...] + below[...]

    @pl.when(jnp.logical_not(mine))
    def _():
        patch[...] = above_in[...] + below[...]


def join(above, above_in, below):
    return pl.pallas_call(
        join_kernel,
        out_shape=jax.ShapeDtypeStruct(below.shape, BF16),
        in_specs=[VMEM] * 3,
        out_specs=VMEM,
        compiler_params=params(8),
        name="join",
    )(above, above_in, below)


def dot(a, b):
    return jnp.dot(a, b, preferred_element_type=F32)


def column_kernel(rows_y, patch_in, *refs):
    weight, turned = refs[:rows_y], refs[rows_y : 2 * rows_y]
    pe, mr, res, sq, inv = refs[2 * rows_y :]
    inner, count = patch_in.shape
    tile = weight[0].shape[1]
    maps = rows_y * tile
    pe[:, pl.ds(0, count)] = patch_in[...]
    patch = patch_in[...]
    for m in range(0, maps, tile):
        r = dot(turned[m // tile][...], patch)
        res[pl.ds(m, tile), :] = r
        mr[pl.ds(m, tile), pl.ds(count, count)] = r.astype(BF16)
        sq[pl.ds(m, tile), :] = r * r
    sq[pl.ds(maps, SUB), :] = sq[pl.ds(0, SUB), :]

    steps = -(-inner // tile)
    for n in range(steps):
        low, high = n * tile, min(inner, (n + 1) * tile)
        rows = pl.ds(low, high - low)
        error = -pe[rows, pl.ds(0, count)].astype(F32)
        for p in range(rows_y):
            error += dot(weight[p][rows, :], mr[pl.ds(p * tile, tile), pl.ds(count, count)])
        pe[rows, pl.ds(count, count)] = error.astype(BF16)
    for m in range(0, maps, tile):
        total = sq[pl.ds(m, tile), :]
        for i in range(1, POOL):
            total = total + sq[pl.ds(m + i, tile), :]
        inv[pl.ds(SUB + m, tile), :] = lax.rsqrt(smoothing + total)
    inv[pl.ds(0, SUB), :] = inv[pl.ds(maps, SUB), :]
    error_b = pe[:, pl.ds(count, count)]
    for m in range(0, maps, tile):
        back = dot(turned[m // tile][...], error_b)
        spread = inv[pl.ds(SUB + m, tile), :]
        for i in range(1, POOL):
            spread = spread + inv[pl.ds(SUB + m - i, tile), :]
        mixed = back + sparsity * res[pl.ds(m, tile), :] * spread
        mr[pl.ds(m, tile), pl.ds(0, count)] = mixed.astype(BF16)


def column(patch, weight, turned):
    inner, count = patch.shape
    rows_y = len(weight)
    maps = rows_y * weight[0].shape[1]
    return pl.pallas_call(
        functools.partial(column_kernel, rows_y),
        out_shape=[
            jax.ShapeDtypeStruct((inner, 2 * count), BF16),
            jax.ShapeDtypeStruct((maps, 2 * count), BF16),
        ],
        in_specs=[VMEM] * (1 + 2 * rows_y),
        out_specs=[VMEM] * 2,
        scratch_shapes=[
            pltpu.VMEM((maps, count), F32),
            pltpu.VMEM((maps + SUB, count), F32),
            pltpu.VMEM((maps + SUB, count), F32),
        ],
        compiler_params=params(40),
        name="column",
    )(patch, *weight, *turned)


def padded(rows):
    return -(-rows // 16) * 16


def piece_kernel(shifts, scale, pe, mr, *refs):
    home, away = refs[-2:]
    inner = pe.shape[0]
    first = lax.rem(lax.axis_index("map"), CORES) == 0
    tile = 256
    for i, p in enumerate(shifts):
        groups = mr[pl.ds(CORES * LANES * p, CORES * LANES), :]
        for n in range(0, inner, tile):
            size = min(tile, inner - n)
            g = lax.dot_general(
                pe[pl.ds(n, size), :], groups, (((1,), (1,)), ((), ())),
                preferred_element_type=F32,
            )
            g = g * scale
            low, high = g[:, :LANES], g[:, LANES:]
            rows = pl.ds(i * padded(inner) + n, size)
            home[rows, :] = jnp.where(first, low, high)
            away[rows, :] = jnp.where(first, high, low).astype(BF16)


def piece(shifts, pe, mr, after=()):
    inner, depth = pe.shape
    rows = len(shifts) * padded(inner)
    return pl.pallas_call(
        functools.partial(piece_kernel, shifts, 1.0 / depth),
        out_shape=[
            jax.ShapeDtypeStruct((rows, LANES), F32),
            jax.ShapeDtypeStruct((rows, LANES), BF16),
        ],
        in_specs=[VMEM] * 2 + [ANY] * len(after),
        out_specs=[VMEM] * 2,
        compiler_params=params(16),
        name="piece",
    )(pe, mr, *after)


def total_kernel(count, home, away, *refs):
    outs = refs[-count:]
    inner = outs[0].shape[0]
    for i, out in enumerate(outs):
        rows = pl.ds(i * padded(inner), inner)
        out[...] = (home[rows, :] + away[rows, :].astype(F32)).astype(BF16)


def total(home, away, count, inner, after):
    return pl.pallas_call(
        functools.partial(total_kernel, count),
        out_shape=[jax.ShapeDtypeStruct((inner, LANES), BF16)] * count,
        in_specs=[VMEM] * 2 + [ANY] * len(after),
        out_specs=[VMEM] * count,
        compiler_params=params(8),
        name="total",
    )(home, away, *after)


def follow_kernel(block, after, out):
    out[...] = block[...]


def follow(block, after):
    return pl.pallas_call(
        follow_kernel,
        out_shape=jax.ShapeDtypeStruct(block.shape, block.dtype),
        in_specs=[VMEM, ANY],
        out_specs=VMEM,
        compiler_params=params(4),
        name="follow",
    )(block, after)


def place_pieces(full, shifts, refs, rows_y, dps):
    y, d = lax.axis_index("map") // CORES, lax.axis_index("dp")
    inner = refs[0].shape[0]
    for n, s in enumerate(shifts):
        row = lax.rem(y + rows_y - s, rows_y)
        for block, part in ((refs[2 * n], d), (refs[2 * n + 1], 1 - d)):
            at = pl.ds(dps * row + part, inner, stride=rows_y * dps)
            full[at, :] = block[...].astype(F32)


def gather_kernel(rows_y, dps, shifts, *refs):
    place_pieces(refs[-1], shifts, refs[:-1], rows_y, dps)


def gather(pieces, shifts, rows_y, dps):
    inner, here = pieces[0].shape
    return pl.pallas_call(
        functools.partial(gather_kernel, rows_y, dps, shifts),
        out_shape=jax.ShapeDtypeStruct((inner * rows_y * dps, here), F32),
        in_specs=[VMEM] * len(pieces),
        out_specs=VMEM,
        compiler_params=params(8),
        name="gather",
    )(*pieces)


def finish_kernel(rows_y, dps, shifts, *refs):
    pieces, weights, early = refs[: 2 * len(shifts)], refs[-8], refs[-7]
    grad, fresh, full, new, grad_sem, sems = refs[-6:]
    full[...] = early[...]
    place_pieces(full, shifts, pieces, rows_y, dps)
    rows = full.shape[0]
    some = rows // dps
    at = pl.multiple_of(lax.axis_index("dp") * some, SUB)
    grad_copy = pltpu.make_async_copy(full.at[pl.ds(at, some), :], grad, grad_sem)
    grad_copy.start()
    copies = []
    for n, low in enumerate(range(0, rows, OUT_ROWS)):
        part = pl.ds(low, min(OUT_ROWS, rows - low))
        new[part, :] = (weights[part, :].astype(F32) - learn_rate * full[part, :]).astype(BF16)
        copy = pltpu.make_async_copy(new.at[part, :], fresh.at[part, :], sems.at[n])
        copy.start()
        copies.append(copy)
    grad_copy.wait()
    for copy in copies:
        copy.wait()


def finish(pieces, shifts, weights, full, rows_y, dps):
    num_cols, inner, here = weights.shape
    rows = inner * num_cols
    flat = weights.transpose(1, 0, 2).reshape(rows, here)
    grad, fresh = pl.pallas_call(
        functools.partial(finish_kernel, rows_y, dps, shifts),
        out_shape=[
            jax.ShapeDtypeStruct((rows // dps, here), F32),
            jax.ShapeDtypeStruct((rows, here), BF16),
        ],
        in_specs=[VMEM] * (len(pieces) + 2),
        out_specs=[HBM, HBM],
        scratch_shapes=[
            pltpu.VMEM((rows, here), F32),
            pltpu.VMEM((rows, here), BF16),
            pltpu.SemaphoreType.DMA,
            pltpu.SemaphoreType.DMA((-(-rows // OUT_ROWS),)),
        ],
        compiler_params=params(16),
        name="finish",
    )(*pieces, flat, full)
    grad = grad.reshape(inner // dps, num_cols, here).transpose(1, 0, 2)
    return grad, fresh.reshape(inner, num_cols, here).transpose(1, 0, 2)


def per_device(mesh_shape, frames, weights, offsets):
    rows_y = mesh_shape[1] // CORES
    def send(x, move):
        return lax.ppermute(x, AXES, table(mesh_shape, move))

    dps = mesh_shape[2]
    places = offsets.T
    upper = send(places, lambda t, y, k, d: (t + 1, y, k, d))
    above, token = cut(frames, places, True)
    below, token = cut(frames, upper, False, (token,))
    own = blocks(weights, rows_y, dps, (token,))
    below = send(below, lambda t, y, k, d: (t - 1, y, d, k))

    weight, turned = [], []
    for s in range(rows_y):
        block = own[s]
        if s:
            block = send(block, lambda t, y, k, d: (t, y - s, k, d))
        other = send(block, lambda t, y, k, d: (t, y, 1 - k, d))
        pair = filters(block, other)
        weight.append(pair[0])
        turned.append(pair[1])
    above_in = send(above, lambda t, y, k, d: (t, y, d, k) if k != d else None)

    pe, mr = column(join(above, above_in, below), weight, turned)

    pieces = {}
    inner = weights.shape[1]
    after_piece, after_total = (), ()
    for shifts in ((0,), (1, 3, 2)):
        home, away = piece(shifts, pe, mr, after_piece)
        after_piece = (away,)
        away = send(away, lambda t, y, k, d: (t, y, 1 - k, d))
        blocks_here = total(home, away, len(shifts), inner, after_total)
        after_total = (blocks_here[0],)
        for s, block in zip(shifts, blocks_here):
            if s:
                block = send(block, lambda t, y, k, d: (t, y + s, k, d))
            if s == 1:
                block = follow(block, pieces[0][1])
            pieces[s] = [block, send(block, lambda t, y, k, d: (t, y, k, 1 - d))]
    early, late = (0, 1, 3), (2,)
    full = gather(sum([pieces[s] for s in early], []), early, rows_y, dps)
    return finish(sum([pieces[s] for s in late], []), late, weights, full, rows_y, dps)


def solution(mesh):
    mesh_shape = tuple(mesh.shape[a] for a in AXES)
    placed = (P(None, "tile", None, "dp"), P("tile", None, "map"), P("tile", None))

    def run(frames, weights, offsets):
        return per_device(mesh_shape, frames, weights, offsets)

    return jax.shard_map(
        run,
        mesh=mesh,
        in_specs=placed,
        out_specs=(P("tile", "dp", "map"), P("tile", None, "map")),
        check_vma=False,
    )
```

```python
import functools

import jax
import jax.numpy as jnp
from jax import lax
from jax.experimental import pallas as pl
from jax.experimental.pallas import tpu as pltpu
from jax.sharding import PartitionSpec as P

FIELD = 18
POOL = 5
CORES = 2
STRIP = 48
SUB = 8
LANES = 128
MIB = 1 << 20
CUT_MIB = 50
OUT_ROWS = 2048

smoothing = 1.0
sparsity = 3.0
learn_rate = 0.1

AXES = ("tile", "map", "dp")
F32, BF16 = jnp.float32, jnp.bfloat16
VMEM = pl.BlockSpec(memory_space=pltpu.VMEM)
SMEM = pl.BlockSpec(memory_space=pltpu.SMEM)
ANY = pl.BlockSpec(memory_space=pl.ANY)
HBM = pl.BlockSpec(memory_space=pltpu.HBM)


def table(mesh_shape, move):
    tiles, maps, dps = mesh_shape
    rows_y = maps // CORES
    pairs = []
    for t in range(tiles):
        for y in range(rows_y):
            for k in range(CORES):
                for d in range(dps):
                    to = move(t, y, k, d)
                    if to is None or not 0 <= to[0] < tiles:
                        continue
                    t2, y2, k2, d2 = to
                    source = (t * maps + y * CORES + k) * dps + d
                    target = (t2 * maps + (y2 % rows_y) * CORES + k2) * dps + d2
                    pairs.append((source, target))
    return pairs


def params(mib):
    return pltpu.CompilerParams(vmem_limit_bytes=mib * MIB)


def cut_kernel(above, places, frames, *refs):
    out, token, strip, wide, flat, sems = refs[-6:]
    channels, rows_here, across, count = frames.shape
    column = lax.axis_index("map")
    top, left = places[0, column], places[1, column]
    base = jnp.minimum(left // 16 * 16, across - STRIP)
    base = pl.multiple_of(base, 16)
    first = jnp.minimum(top, rows_here - FIELD) if above else 0
    copies = [
        pltpu.make_async_copy(
            frames.at[channel, pl.ds(first, FIELD), pl.ds(base, STRIP), :],
            strip.at[channel],
            sems.at[channel],
        )
        for channel in range(channels)
    ]
    for copy in copies:
        copy.start()
    token[...] = jnp.zeros_like(token)
    shift = left - base
    for channel in range(channels):
        copies[channel].wait()
        for n in range(count // LANES):
            lanes = strip[channel, :, :, pl.ds(n * LANES, LANES)]
            wide[n] = lanes.reshape(FIELD * STRIP, LANES).astype(F32)
        for r in range(FIELD):
            row = top + r - (first if above else rows_here)
            valid = (row < FIELD) if above else (row >= 0)
            row = jnp.clip(row, 0, FIELD - 1)
            for n in range(count // LANES):
                x = wide[n, pl.ds(row * STRIP + shift, FIELD), :]
                x = jnp.where(valid, x, 0.0)
                at = pl.ds((channel * FIELD + r) * FIELD, FIELD)
                flat[at, pl.ds(n * LANES, LANES)] = x
    inner = channels * FIELD * FIELD
    out[...] = flat[pl.ds(0, inner), :].astype(BF16)


def cut(frames, places, above, after=()):
    channels, rows_here, wide, count = frames.shape
    inner = channels * FIELD * FIELD
    return pl.pallas_call(
        functools.partial(cut_kernel, above),
        out_shape=[
            jax.ShapeDtypeStruct((inner, count), BF16),
            jax.ShapeDtypeStruct((SUB, LANES), F32),
        ],
        in_specs=[SMEM, HBM] + [ANY] * len(after),
        out_specs=[VMEM] * 2,
        scratch_shapes=[
            pltpu.VMEM((channels, FIELD, STRIP, count), BF16),
            pltpu.VMEM((count // LANES, FIELD * STRIP, LANES), F32),
            pltpu.VMEM((inner, count), F32),
            pltpu.SemaphoreType.DMA((channels,)),
        ],
        compiler_params=params(CUT_MIB),
        name="cut_above" if above else "cut_below",
    )(places, frames, *after)


def blocks_kernel(rows_y, dps, flat, *refs):
    outs, wide = refs[-1 - rows_y : -1], refs[-1]
    inner = outs[0].shape[0]
    y, d = lax.axis_index("map") // CORES, lax.axis_index("dp")
    wide[...] = flat[...].astype(F32)
    for s in range(rows_y):
        column = dps * lax.rem(y + rows_y - s, rows_y) + d
        outs[s][...] = wide[pl.ds(column, inner, stride=rows_y * dps), :].astype(BF16)


def blocks(weights, rows_y, dps, after=()):
    num_cols, inner, here = weights.shape
    flat = weights.transpose(1, 0, 2).reshape(inner * num_cols, here)
    return pl.pallas_call(
        functools.partial(blocks_kernel, rows_y, dps),
        out_shape=[jax.ShapeDtypeStruct((inner, here), BF16)] * rows_y,
        in_specs=[VMEM] + [ANY] * len(after),
        out_specs=[VMEM] * rows_y,
        scratch_shapes=[pltpu.VMEM(flat.shape, F32)],
        compiler_params=params(16),
        name="blocks",
    )(flat, *after)


def filters_kernel(own, other, weight, turned):
    k = lax.rem(lax.axis_index("map"), CORES)
    for block, core in ((own[...], k), (other[...], 1 - k)):
        at = pl.multiple_of(core * LANES, LANES)
        weight[:, pl.ds(at, LANES)] = block
        turned[pl.ds(at, LANES), :] = block.T


def filters(own, other):
    inner, here = own.shape
    return pl.pallas_call(
        filters_kernel,
        out_shape=[
            jax.ShapeDtypeStruct((inner, CORES * here), BF16),
            jax.ShapeDtypeStruct((CORES * here, inner), BF16),
        ],
        in_specs=[VMEM] * 2,
        out_specs=[VMEM] * 2,
        compiler_params=params(8),
        name="filters",
    )(own, other)


def join_kernel(above, above_in, below, patch):
    mine = lax.rem(lax.axis_index("map"), CORES) == lax.axis_index("dp")

    @pl.when(mine)
    def _():
        patch[...] = above[...] + below[...]

    @pl.when(jnp.logical_not(mine))
    def _():
        patch[...] = above_in[...] + below[...]


def join(above, above_in, below):
    return pl.pallas_call(
        join_kernel,
        out_shape=jax.ShapeDtypeStruct(below.shape, BF16),
        in_specs=[VMEM] * 3,
        out_specs=VMEM,
        compiler_params=params(8),
        name="join",
    )(above, above_in, below)


def dot(a, b):
    return jnp.dot(a, b, preferred_element_type=F32)


def column_kernel(rows_y, patch_in, *refs):
    weight, turned = refs[:rows_y], refs[rows_y : 2 * rows_y]
    pe, mr, res, sq, inv = refs[2 * rows_y :]
    inner, count = patch_in.shape
    tile = weight[0].shape[1]
    maps = rows_y * tile
    pe[:, pl.ds(0, count)] = patch_in[...]
    patch = patch_in[...]
    for m in range(0, maps, tile):
        r = dot(turned[m // tile][...], patch)
        res[pl.ds(m, tile), :] = r
        mr[pl.ds(m, tile), pl.ds(count, count)] = r.astype(BF16)
        sq[pl.ds(m, tile), :] = r * r
    sq[pl.ds(maps, SUB), :] = sq[pl.ds(0, SUB), :]

    steps = -(-inner // tile)
    for n in range(steps):
        low, high = n * tile, min(inner, (n + 1) * tile)
        rows = pl.ds(low, high - low)
        error = -pe[rows, pl.ds(0, count)].astype(F32)
        for p in range(rows_y):
            error += dot(weight[p][rows, :], mr[pl.ds(p * tile, tile), pl.ds(count, count)])
        pe[rows, pl.ds(count, count)] = error.astype(BF16)
    for m in range(0, maps, tile):
        total = sq[pl.ds(m, tile), :]
        for i in range(1, POOL):
            total = total + sq[pl.ds(m + i, tile), :]
        inv[pl.ds(SUB + m, tile), :] = lax.rsqrt(smoothing + total)
    inv[pl.ds(0, SUB), :] = inv[pl.ds(maps, SUB), :]
    error_b = pe[:, pl.ds(count, count)]
    for m in range(0, maps, tile):
        back = dot(turned[m // tile][...], error_b)
        spread = inv[pl.ds(SUB + m, tile), :]
        for i in range(1, POOL):
            spread = spread + inv[pl.ds(SUB + m - i, tile), :]
        mixed = back + sparsity * res[pl.ds(m, tile), :] * spread
        mr[pl.ds(m, tile), pl.ds(0, count)] = mixed.astype(BF16)


def column(patch, weight, turned):
    inner, count = patch.shape
    rows_y = len(weight)
    maps = rows_y * weight[0].shape[1]
    return pl.pallas_call(
        functools.partial(column_kernel, rows_y),
        out_shape=[
            jax.ShapeDtypeStruct((inner, 2 * count), BF16),
            jax.ShapeDtypeStruct((maps, 2 * count), BF16),
        ],
        in_specs=[VMEM] * (1 + 2 * rows_y),
        out_specs=[VMEM] * 2,
        scratch_shapes=[
            pltpu.VMEM((maps, count), F32),
            pltpu.VMEM((maps + SUB, count), F32),
            pltpu.VMEM((maps + SUB, count), F32),
        ],
        compiler_params=params(40),
        name="column",
    )(patch, *weight, *turned)


def padded(rows):
    return -(-rows // 16) * 16


def piece_kernel(shifts, scale, pe, mr, *refs):
    home, away = refs[-2:]
    inner = pe.shape[0]
    first = lax.rem(lax.axis_index("map"), CORES) == 0
    tile = 256
    for i, p in enumerate(shifts):
        groups = mr[pl.ds(CORES * LANES * p, CORES * LANES), :]
        for n in range(0, inner, tile):
            size = min(tile, inner - n)
            g = lax.dot_general(
                pe[pl.ds(n, size), :], groups, (((1,), (1,)), ((), ())),
                preferred_element_type=F32,
            )
            g = g * scale
            low, high = g[:, :LANES], g[:, LANES:]
            rows = pl.ds(i * padded(inner) + n, size)
            home[rows, :] = jnp.where(first, low, high)
            away[rows, :] = jnp.where(first, high, low).astype(BF16)


def piece(shifts, pe, mr, after=()):
    inner, depth = pe.shape
    rows = len(shifts) * padded(inner)
    return pl.pallas_call(
        functools.partial(piece_kernel, shifts, 1.0 / depth),
        out_shape=[
            jax.ShapeDtypeStruct((rows, LANES), F32),
            jax.ShapeDtypeStruct((rows, LANES), BF16),
        ],
        in_specs=[VMEM] * 2 + [ANY] * len(after),
        out_specs=[VMEM] * 2,
        compiler_params=params(16),
        name="piece",
    )(pe, mr, *after)


def total_kernel(count, home, away, *refs):
    outs = refs[-count:]
    inner = outs[0].shape[0]
    for i, out in enumerate(outs):
        rows = pl.ds(i * padded(inner), inner)
        out[...] = (home[rows, :] + away[rows, :].astype(F32)).astype(BF16)


def total(home, away, count, inner, after):
    return pl.pallas_call(
        functools.partial(total_kernel, count),
        out_shape=[jax.ShapeDtypeStruct((inner, LANES), BF16)] * count,
        in_specs=[VMEM] * 2 + [ANY] * len(after),
        out_specs=[VMEM] * count,
        compiler_params=params(8),
        name="total",
    )(home, away, *after)


def follow_kernel(block, after, out):
    out[...] = block[...]


def follow(block, after):
    return pl.pallas_call(
        follow_kernel,
        out_shape=jax.ShapeDtypeStruct(block.shape, block.dtype),
        in_specs=[VMEM, ANY],
        out_specs=VMEM,
        compiler_params=params(4),
        name="follow",
    )(block, after)


def place_pieces(full, shifts, refs, rows_y, dps):
    y, d = lax.axis_index("map") // CORES, lax.axis_index("dp")
    inner = refs[0].shape[0]
    for n, s in enumerate(shifts):
        row = lax.rem(y + rows_y - s, rows_y)
        for block, part in ((refs[2 * n], d), (refs[2 * n + 1], 1 - d)):
            at = pl.ds(dps * row + part, inner, stride=rows_y * dps)
            full[at, :] = block[...].astype(F32)


def gather_kernel(rows_y, dps, shifts, *refs):
    place_pieces(refs[-1], shifts, refs[:-1], rows_y, dps)


def gather(pieces, shifts, rows_y, dps):
    inner, here = pieces[0].shape
    return pl.pallas_call(
        functools.partial(gather_kernel, rows_y, dps, shifts),
        out_shape=jax.ShapeDtypeStruct((inner * rows_y * dps, here), F32),
        in_specs=[VMEM] * len(pieces),
        out_specs=VMEM,
        compiler_params=params(8),
        name="gather",
    )(*pieces)


def finish_kernel(rows_y, dps, shifts, *refs):
    pieces, weights, early = refs[: 2 * len(shifts)], refs[-8], refs[-7]
    grad, fresh, full, new, grad_sem, sems = refs[-6:]
    full[...] = early[...]
    place_pieces(full, shifts, pieces, rows_y, dps)
    rows = full.shape[0]
    some = rows // dps
    at = pl.multiple_of(lax.axis_index("dp") * some, SUB)
    grad_copy = pltpu.make_async_copy(full.at[pl.ds(at, some), :], grad, grad_sem)
    grad_copy.start()
    copies = []
    for n, low in enumerate(range(0, rows, OUT_ROWS)):
        part = pl.ds(low, min(OUT_ROWS, rows - low))
        new[part, :] = (weights[part, :].astype(F32) - learn_rate * full[part, :]).astype(BF16)
        copy = pltpu.make_async_copy(new.at[part, :], fresh.at[part, :], sems.at[n])
        copy.start()
        copies.append(copy)
    grad_copy.wait()
    for copy in copies:
        copy.wait()


def finish(pieces, shifts, weights, full, rows_y, dps):
    num_cols, inner, here = weights.shape
    rows = inner * num_cols
    flat = weights.transpose(1, 0, 2).reshape(rows, here)
    grad, fresh = pl.pallas_call(
        functools.partial(finish_kernel, rows_y, dps, shifts),
        out_shape=[
            jax.ShapeDtypeStruct((rows // dps, here), F32),
            jax.ShapeDtypeStruct((rows, here), BF16),
        ],
        in_specs=[VMEM] * (len(pieces) + 2),
        out_specs=[HBM, HBM],
        scratch_shapes=[
            pltpu.VMEM((rows, here), F32),
            pltpu.VMEM((rows, here), BF16),
            pltpu.SemaphoreType.DMA,
            pltpu.SemaphoreType.DMA((-(-rows // OUT_ROWS),)),
        ],
        compiler_params=params(16),
        name="finish",
    )(*pieces, flat, full)
    grad = grad.reshape(inner // dps, num_cols, here).transpose(1, 0, 2)
    return grad, fresh.reshape(inner, num_cols, here).transpose(1, 0, 2)


def per_device(mesh_shape, frames, weights, offsets):
    rows_y = mesh_shape[1] // CORES
    def send(x, move):
        return lax.ppermute(x, AXES, table(mesh_shape, move))

    dps = mesh_shape[2]
    places = offsets.T
    upper = send(places, lambda t, y, k, d: (t + 1, y, k, d))
    above, token = cut(frames, places, True)
    below, token = cut(frames, upper, False, (token,))
    own = blocks(weights, rows_y, dps, (token,))
    below = send(below, lambda t, y, k, d: (t - 1, y, d, k))

    weight, turned = [], []
    for s in range(rows_y):
        block = own[s]
        if s:
            block = send(block, lambda t, y, k, d: (t, y - s, k, d))
        other = send(block, lambda t, y, k, d: (t, y, 1 - k, d))
        pair = filters(block, other)
        weight.append(pair[0])
        turned.append(pair[1])
    above_in = send(above, lambda t, y, k, d: (t, y, d, k) if k != d else None)

    pe, mr = column(join(above, above_in, below), weight, turned)

    pieces = {}
    inner = weights.shape[1]
    after_piece, after_total = (), ()
    for shifts in ((0,), (1, 3, 2)):
        home, away = piece(shifts, pe, mr, after_piece)
        after_piece = (away,)
        away = send(away, lambda t, y, k, d: (t, y, 1 - k, d))
        blocks_here = total(home, away, len(shifts), inner, after_total)
        after_total = (blocks_here[0],)
        for s, block in zip(shifts, blocks_here):
            if s == 2:
                block = follow(block, first)
            if s:
                block = send(block, lambda t, y, k, d: (t, y + s, k, d))
            if s == 1:
                first = block
                block = follow(block, pieces[0][1])
            pieces[s] = [block, send(block, lambda t, y, k, d: (t, y, k, 1 - d))]
    early, late = (0, 1, 3), (2,)
    full = gather(sum([pieces[s] for s in early], []), early, rows_y, dps)
    return finish(sum([pieces[s] for s in late], []), late, weights, full, rows_y, dps)


def solution(mesh):
    mesh_shape = tuple(mesh.shape[a] for a in AXES)
    placed = (P(None, "tile", None, "dp"), P("tile", None, "map"), P("tile", None))

    def run(frames, weights, offsets):
        return per_device(mesh_shape, frames, weights, offsets)

    return jax.shard_map(
        run,
        mesh=mesh,
        in_specs=placed,
        out_specs=(P("tile", "dp", "map"), P("tile", None, "map")),
        check_vma=False,
    )
```

```python
import functools

import jax
import jax.numpy as jnp
from jax import lax
from jax.experimental import pallas as pl
from jax.experimental.pallas import tpu as pltpu
from jax.sharding import PartitionSpec as P

FIELD = 18
POOL = 5
CORES = 2
STRIP = 48
SUB = 8
LANES = 128
MIB = 1 << 20
CUT_MIB = 50
OUT_ROWS = 2048

smoothing = 1.0
sparsity = 3.0
learn_rate = 0.1

AXES = ("tile", "map", "dp")
F32, BF16 = jnp.float32, jnp.bfloat16
VMEM = pl.BlockSpec(memory_space=pltpu.VMEM)
SMEM = pl.BlockSpec(memory_space=pltpu.SMEM)
ANY = pl.BlockSpec(memory_space=pl.ANY)
HBM = pl.BlockSpec(memory_space=pltpu.HBM)


def table(mesh_shape, move):
    tiles, maps, dps = mesh_shape
    rows_y = maps // CORES
    pairs = []
    for t in range(tiles):
        for y in range(rows_y):
            for k in range(CORES):
                for d in range(dps):
                    to = move(t, y, k, d)
                    if to is None or not 0 <= to[0] < tiles:
                        continue
                    t2, y2, k2, d2 = to
                    source = (t * maps + y * CORES + k) * dps + d
                    target = (t2 * maps + (y2 % rows_y) * CORES + k2) * dps + d2
                    pairs.append((source, target))
    return pairs


def params(mib):
    return pltpu.CompilerParams(vmem_limit_bytes=mib * MIB)


def cut_kernel(above, places, frames, *refs):
    out, token, strip, wide, flat, sems = refs[-6:]
    channels, rows_here, across, count = frames.shape
    column = lax.axis_index("map")
    top, left = places[0, column], places[1, column]
    base = jnp.minimum(left // 16 * 16, across - STRIP)
    base = pl.multiple_of(base, 16)
    first = jnp.minimum(top, rows_here - FIELD) if above else 0
    copies = [
        pltpu.make_async_copy(
            frames.at[channel, pl.ds(first, FIELD), pl.ds(base, STRIP), :],
            strip.at[channel],
            sems.at[channel],
        )
        for channel in range(channels)
    ]
    for copy in copies:
        copy.start()
    token[...] = jnp.zeros_like(token)
    shift = left - base
    for channel in range(channels):
        copies[channel].wait()
        for n in range(count // LANES):
            lanes = strip[channel, :, :, pl.ds(n * LANES, LANES)]
            wide[n] = lanes.reshape(FIELD * STRIP, LANES).astype(F32)
        for r in range(FIELD):
            row = top + r - (first if above else rows_here)
            valid = (row < FIELD) if above else (row >= 0)
            row = jnp.clip(row, 0, FIELD - 1)
            for n in range(count // LANES):
                x = wide[n, pl.ds(row * STRIP + shift, FIELD), :]
                x = jnp.where(valid, x, 0.0)
                at = pl.ds((channel * FIELD + r) * FIELD, FIELD)
                flat[at, pl.ds(n * LANES, LANES)] = x
    inner = channels * FIELD * FIELD
    out[...] = flat[pl.ds(0, inner), :].astype(BF16)


def cut(frames, places, above, after=()):
    channels, rows_here, wide, count = frames.shape
    inner = channels * FIELD * FIELD
    return pl.pallas_call(
        functools.partial(cut_kernel, above),
        out_shape=[
            jax.ShapeDtypeStruct((inner, count), BF16),
            jax.ShapeDtypeStruct((SUB, LANES), F32),
        ],
        in_specs=[SMEM, HBM] + [ANY] * len(after),
        out_specs=[VMEM] * 2,
        scratch_shapes=[
            pltpu.VMEM((channels, FIELD, STRIP, count), BF16),
            pltpu.VMEM((count // LANES, FIELD * STRIP, LANES), F32),
            pltpu.VMEM((inner, count), F32),
            pltpu.SemaphoreType.DMA((channels,)),
        ],
        compiler_params=params(CUT_MIB),
        name="cut_above" if above else "cut_below",
    )(places, frames, *after)


def blocks_kernel(rows_y, dps, flat, *refs):
    outs, wide = refs[-1 - rows_y : -1], refs[-1]
    inner = outs[0].shape[0]
    y, d = lax.axis_index("map") // CORES, lax.axis_index("dp")
    wide[...] = flat[...].astype(F32)
    for s in range(rows_y):
        column = dps * lax.rem(y + rows_y - s, rows_y) + d
        outs[s][...] = wide[pl.ds(column, inner, stride=rows_y * dps), :].astype(BF16)


def blocks(weights, rows_y, dps, after=()):
    num_cols, inner, here = weights.shape
    flat = weights.transpose(1, 0, 2).reshape(inner * num_cols, here)
    return pl.pallas_call(
        functools.partial(blocks_kernel, rows_y, dps),
        out_shape=[jax.ShapeDtypeStruct((inner, here), BF16)] * rows_y,
        in_specs=[VMEM] + [ANY] * len(after),
        out_specs=[VMEM] * rows_y,
        scratch_shapes=[pltpu.VMEM(flat.shape, F32)],
        compiler_params=params(16),
        name="blocks",
    )(flat, *after)


def filters_kernel(own, other, weight, turned):
    k = lax.rem(lax.axis_index("map"), CORES)
    for block, core in ((own[...], k), (other[...], 1 - k)):
        at = pl.multiple_of(core * LANES, LANES)
        weight[:, pl.ds(at, LANES)] = block
        turned[pl.ds(at, LANES), :] = block.T


def filters(own, other):
    inner, here = own.shape
    return pl.pallas_call(
        filters_kernel,
        out_shape=[
            jax.ShapeDtypeStruct((inner, CORES * here), BF16),
            jax.ShapeDtypeStruct((CORES * here, inner), BF16),
        ],
        in_specs=[VMEM] * 2,
        out_specs=[VMEM] * 2,
        compiler_params=params(8),
        name="filters",
    )(own, other)


def join_kernel(above, above_in, below, patch):
    mine = lax.rem(lax.axis_index("map"), CORES) == lax.axis_index("dp")

    @pl.when(mine)
    def _():
        patch[...] = above[...] + below[...]

    @pl.when(jnp.logical_not(mine))
    def _():
        patch[...] = above_in[...] + below[...]


def join(above, above_in, below):
    return pl.pallas_call(
        join_kernel,
        out_shape=jax.ShapeDtypeStruct(below.shape, BF16),
        in_specs=[VMEM] * 3,
        out_specs=VMEM,
        compiler_params=params(8),
        name="join",
    )(above, above_in, below)


def dot(a, b):
    return jnp.dot(a, b, preferred_element_type=F32)


def column_kernel(rows_y, patch_in, *refs):
    weight, turned = refs[:rows_y], refs[rows_y : 2 * rows_y]
    pe, mr, res, sq, inv = refs[2 * rows_y :]
    inner, count = patch_in.shape
    tile = weight[0].shape[1]
    maps = rows_y * tile
    pe[:, pl.ds(0, count)] = patch_in[...]
    patch = patch_in[...]
    for m in range(0, maps, tile):
        r = dot(turned[m // tile][...], patch)
        res[pl.ds(m, tile), :] = r
        mr[pl.ds(m, tile), pl.ds(count, count)] = r.astype(BF16)
        sq[pl.ds(m, tile), :] = r * r
    sq[pl.ds(maps, SUB), :] = sq[pl.ds(0, SUB), :]

    steps = -(-inner // tile)
    for n in range(steps):
        low, high = n * tile, min(inner, (n + 1) * tile)
        rows = pl.ds(low, high - low)
        error = -pe[rows, pl.ds(0, count)].astype(F32)
        for p in range(rows_y):
            error += dot(weight[p][rows, :], mr[pl.ds(p * tile, tile), pl.ds(count, count)])
        pe[rows, pl.ds(count, count)] = error.astype(BF16)
    for m in range(0, maps, tile):
        total = sq[pl.ds(m, tile), :]
        for i in range(1, POOL):
            total = total + sq[pl.ds(m + i, tile), :]
        inv[pl.ds(SUB + m, tile), :] = lax.rsqrt(smoothing + total)
    inv[pl.ds(0, SUB), :] = inv[pl.ds(maps, SUB), :]
    error_b = pe[:, pl.ds(count, count)]
    for m in range(0, maps, tile):
        back = dot(turned[m // tile][...], error_b)
        spread = inv[pl.ds(SUB + m, tile), :]
        for i in range(1, POOL):
            spread = spread + inv[pl.ds(SUB + m - i, tile), :]
        mixed = back + sparsity * res[pl.ds(m, tile), :] * spread
        mr[pl.ds(m, tile), pl.ds(0, count)] = mixed.astype(BF16)


def column(patch, weight, turned):
    inner, count = patch.shape
    rows_y = len(weight)
    maps = rows_y * weight[0].shape[1]
    return pl.pallas_call(
        functools.partial(column_kernel, rows_y),
        out_shape=[
            jax.ShapeDtypeStruct((inner, 2 * count), BF16),
            jax.ShapeDtypeStruct((maps, 2 * count), BF16),
        ],
        in_specs=[VMEM] * (1 + 2 * rows_y),
        out_specs=[VMEM] * 2,
        scratch_shapes=[
            pltpu.VMEM((maps, count), F32),
            pltpu.VMEM((maps + SUB, count), F32),
            pltpu.VMEM((maps + SUB, count), F32),
        ],
        compiler_params=params(40),
        name="column",
    )(patch, *weight, *turned)


def padded(rows):
    return -(-rows // 16) * 16


def piece_kernel(shifts, scale, pe, mr, *refs):
    home, away = refs[-2:]
    inner = pe.shape[0]
    first = lax.rem(lax.axis_index("map"), CORES) == 0
    tile = 256
    for i, p in enumerate(shifts):
        groups = mr[pl.ds(CORES * LANES * p, CORES * LANES), :]
        for n in range(0, inner, tile):
            size = min(tile, inner - n)
            g = lax.dot_general(
                pe[pl.ds(n, size), :], groups, (((1,), (1,)), ((), ())),
                preferred_element_type=F32,
            )
            g = g * scale
            low, high = g[:, :LANES], g[:, LANES:]
            rows = pl.ds(i * padded(inner) + n, size)
            home[rows, :] = jnp.where(first, low, high)
            away[rows, :] = jnp.where(first, high, low).astype(BF16)


def piece(shifts, pe, mr, after=()):
    inner, depth = pe.shape
    rows = len(shifts) * padded(inner)
    return pl.pallas_call(
        functools.partial(piece_kernel, shifts, 1.0 / depth),
        out_shape=[
            jax.ShapeDtypeStruct((rows, LANES), F32),
            jax.ShapeDtypeStruct((rows, LANES), BF16),
        ],
        in_specs=[VMEM] * 2 + [ANY] * len(after),
        out_specs=[VMEM] * 2,
        compiler_params=params(16),
        name="piece",
    )(pe, mr, *after)


def total_kernel(count, home, away, *refs):
    outs = refs[-count:]
    inner = outs[0].shape[0]
    for i, out in enumerate(outs):
        rows = pl.ds(i * padded(inner), inner)
        out[...] = (home[rows, :] + away[rows, :].astype(F32)).astype(BF16)


def total(home, away, count, inner, after):
    return pl.pallas_call(
        functools.partial(total_kernel, count),
        out_shape=[jax.ShapeDtypeStruct((inner, LANES), BF16)] * count,
        in_specs=[VMEM] * 2 + [ANY] * len(after),
        out_specs=[VMEM] * count,
        compiler_params=params(8),
        name="total",
    )(home, away, *after)


def follow_kernel(block, after, out):
    out[...] = block[...]


def follow(block, after):
    return pl.pallas_call(
        follow_kernel,
        out_shape=jax.ShapeDtypeStruct(block.shape, block.dtype),
        in_specs=[VMEM, ANY],
        out_specs=VMEM,
        compiler_params=params(4),
        name="follow",
    )(block, after)


def place_pieces(full, shifts, refs, rows_y, dps):
    y, d = lax.axis_index("map") // CORES, lax.axis_index("dp")
    inner = refs[0].shape[0]
    for n, s in enumerate(shifts):
        row = lax.rem(y + rows_y - s, rows_y)
        for block, part in ((refs[2 * n], d), (refs[2 * n + 1], 1 - d)):
            at = pl.ds(dps * row + part, inner, stride=rows_y * dps)
            full[at, :] = block[...].astype(F32)


def gather_kernel(rows_y, dps, shifts, *refs):
    place_pieces(refs[-1], shifts, refs[:-1], rows_y, dps)


def gather(pieces, shifts, rows_y, dps):
    inner, here = pieces[0].shape
    return pl.pallas_call(
        functools.partial(gather_kernel, rows_y, dps, shifts),
        out_shape=jax.ShapeDtypeStruct((inner * rows_y * dps, here), F32),
        in_specs=[VMEM] * len(pieces),
        out_specs=VMEM,
        compiler_params=params(8),
        name="gather",
    )(*pieces)


def finish_kernel(rows_y, dps, shifts, *refs):
    pieces, weights, early = refs[: 2 * len(shifts)], refs[-8], refs[-7]
    grad, fresh, full, new, grad_sem, sems = refs[-6:]
    full[...] = early[...]
    place_pieces(full, shifts, pieces, rows_y, dps)
    rows = full.shape[0]
    some = rows // dps
    at = pl.multiple_of(lax.axis_index("dp") * some, SUB)
    grad_copy = pltpu.make_async_copy(full.at[pl.ds(at, some), :], grad, grad_sem)
    grad_copy.start()
    copies = []
    for n, low in enumerate(range(0, rows, OUT_ROWS)):
        part = pl.ds(low, min(OUT_ROWS, rows - low))
        new[part, :] = (weights[part, :].astype(F32) - learn_rate * full[part, :]).astype(BF16)
        copy = pltpu.make_async_copy(new.at[part, :], fresh.at[part, :], sems.at[n])
        copy.start()
        copies.append(copy)
    grad_copy.wait()
    for copy in copies:
        copy.wait()


def finish(pieces, shifts, weights, full, rows_y, dps):
    num_cols, inner, here = weights.shape
    rows = inner * num_cols
    flat = weights.transpose(1, 0, 2).reshape(rows, here)
    grad, fresh = pl.pallas_call(
        functools.partial(finish_kernel, rows_y, dps, shifts),
        out_shape=[
            jax.ShapeDtypeStruct((rows // dps, here), F32),
            jax.ShapeDtypeStruct((rows, here), BF16),
        ],
        in_specs=[VMEM] * (len(pieces) + 2),
        out_specs=[HBM, HBM],
        scratch_shapes=[
            pltpu.VMEM((rows, here), F32),
            pltpu.VMEM((rows, here), BF16),
            pltpu.SemaphoreType.DMA,
            pltpu.SemaphoreType.DMA((-(-rows // OUT_ROWS),)),
        ],
        compiler_params=params(16),
        name="finish",
    )(*pieces, flat, full)
    grad = grad.reshape(inner // dps, num_cols, here).transpose(1, 0, 2)
    return grad, fresh.reshape(inner, num_cols, here).transpose(1, 0, 2)


def per_device(mesh_shape, frames, weights, offsets):
    rows_y = mesh_shape[1] // CORES
    def send(x, move):
        return lax.ppermute(x, AXES, table(mesh_shape, move))

    dps = mesh_shape[2]
    places = offsets.T
    upper = send(places, lambda t, y, k, d: (t + 1, y, k, d))
    below, token = cut(frames, upper, False)
    own = blocks(weights, rows_y, dps, (token,))
    below = send(below, lambda t, y, k, d: (t - 1, y, d, k))

    weight, turned = [], []
    for s in range(rows_y):
        block = own[s]
        if s:
            block = send(block, lambda t, y, k, d: (t, y - s, k, d))
        other = send(block, lambda t, y, k, d: (t, y, 1 - k, d))
        pair = filters(block, other)
        weight.append(pair[0])
        turned.append(pair[1])
        if s == 0:
            above, _ = cut(frames, places, True, (other,))
    above_in = send(above, lambda t, y, k, d: (t, y, d, k) if k != d else None)
    above_in = send(above, lambda t, y, k, d: (t, y, d, k) if k != d else None)

    pe, mr = column(join(above, above_in, below), weight, turned)

    pieces = {}
    inner = weights.shape[1]
    after_piece, after_total = (), ()
    for shifts in ((0,), (1, 3, 2)):
        home, away = piece(shifts, pe, mr, after_piece)
        after_piece = (away,)
        away = send(away, lambda t, y, k, d: (t, y, 1 - k, d))
        blocks_here = total(home, away, len(shifts), inner, after_total)
        after_total = (blocks_here[0],)
        for s, block in zip(shifts, blocks_here):
            if s == 2:
                block = follow(block, pieces[0][1])
            if s:
                block = send(block, lambda t, y, k, d: (t, y + s, k, d))
            pieces[s] = [block, send(block, lambda t, y, k, d: (t, y, k, 1 - d))]
    early, late = (0, 1, 3), (2,)
    full = gather(sum([pieces[s] for s in early], []), early, rows_y, dps)
    return finish(sum([pieces[s] for s in late], []), late, weights, full, rows_y, dps)


def solution(mesh):
    mesh_shape = tuple(mesh.shape[a] for a in AXES)
    placed = (P(None, "tile", None, "dp"), P("tile", None, "map"), P("tile", None))

    def run(frames, weights, offsets):
        return per_device(mesh_shape, frames, weights, offsets)

    return jax.shard_map(
        run,
        mesh=mesh,
        in_specs=placed,
        out_specs=(P("tile", "dp", "map"), P("tile", None, "map")),
        check_vma=False,
    )
```

```python
import functools

import jax
import jax.numpy as jnp
from jax import lax
from jax.experimental import pallas as pl
from jax.experimental.pallas import tpu as pltpu
from jax.sharding import PartitionSpec as P

FIELD = 18
POOL = 5
CORES = 2
STRIP = 48
SUB = 8
LANES = 128
MIB = 1 << 20
CUT_MIB = 50
OUT_ROWS = 2048

smoothing = 1.0
sparsity = 3.0
learn_rate = 0.1

AXES = ("tile", "map", "dp")
F32, BF16 = jnp.float32, jnp.bfloat16
VMEM = pl.BlockSpec(memory_space=pltpu.VMEM)
SMEM = pl.BlockSpec(memory_space=pltpu.SMEM)
ANY = pl.BlockSpec(memory_space=pl.ANY)
HBM = pl.BlockSpec(memory_space=pltpu.HBM)


def table(mesh_shape, move):
    tiles, maps, dps = mesh_shape
    rows_y = maps // CORES
    pairs = []
    for t in range(tiles):
        for y in range(rows_y):
            for k in range(CORES):
                for d in range(dps):
                    to = move(t, y, k, d)
                    if to is None or not 0 <= to[0] < tiles:
                        continue
                    t2, y2, k2, d2 = to
                    source = (t * maps + y * CORES + k) * dps + d
                    target = (t2 * maps + (y2 % rows_y) * CORES + k2) * dps + d2
                    pairs.append((source, target))
    return pairs


def params(mib):
    return pltpu.CompilerParams(vmem_limit_bytes=mib * MIB)


def cut_kernel(above, places, frames, *refs):
    out, token, strip, wide, flat, sems = refs[-6:]
    channels, rows_here, across, count = frames.shape
    column = lax.axis_index("map")
    top, left = places[0, column], places[1, column]
    base = jnp.minimum(left // 16 * 16, across - STRIP)
    base = pl.multiple_of(base, 16)
    first = jnp.minimum(top, rows_here - FIELD) if above else 0
    copies = [
        pltpu.make_async_copy(
            frames.at[channel, pl.ds(first, FIELD), pl.ds(base, STRIP), :],
            strip.at[channel],
            sems.at[channel],
        )
        for channel in range(channels)
    ]
    for copy in copies:
        copy.start()
    token[...] = jnp.zeros_like(token)
    shift = left - base
    for channel in range(channels):
        copies[channel].wait()
        for n in range(count // LANES):
            lanes = strip[channel, :, :, pl.ds(n * LANES, LANES)]
            wide[n] = lanes.reshape(FIELD * STRIP, LANES).astype(F32)
        for r in range(FIELD):
            row = top + r - (first if above else rows_here)
            valid = (row < FIELD) if above else (row >= 0)
            row = jnp.clip(row, 0, FIELD - 1)
            for n in range(count // LANES):
                x = wide[n, pl.ds(row * STRIP + shift, FIELD), :]
                x = jnp.where(valid, x, 0.0)
                at = pl.ds((channel * FIELD + r) * FIELD, FIELD)
                flat[at, pl.ds(n * LANES, LANES)] = x
    inner = channels * FIELD * FIELD
    out[...] = flat[pl.ds(0, inner), :].astype(BF16)


def cut(frames, places, above, after=()):
    channels, rows_here, wide, count = frames.shape
    inner = channels * FIELD * FIELD
    return pl.pallas_call(
        functools.partial(cut_kernel, above),
        out_shape=[
            jax.ShapeDtypeStruct((inner, count), BF16),
            jax.ShapeDtypeStruct((SUB, LANES), F32),
        ],
        in_specs=[SMEM, HBM] + [ANY] * len(after),
        out_specs=[VMEM] * 2,
        scratch_shapes=[
            pltpu.VMEM((channels, FIELD, STRIP, count), BF16),
            pltpu.VMEM((count // LANES, FIELD * STRIP, LANES), F32),
            pltpu.VMEM((inner, count), F32),
            pltpu.SemaphoreType.DMA((channels,)),
        ],
        compiler_params=params(CUT_MIB),
        name="cut_above" if above else "cut_below",
    )(places, frames, *after)


def blocks_kernel(rows_y, dps, flat, *refs):
    outs, wide = refs[-1 - rows_y : -1], refs[-1]
    inner = outs[0].shape[0]
    y, d = lax.axis_index("map") // CORES, lax.axis_index("dp")
    wide[...] = flat[...].astype(F32)
    for s in range(rows_y):
        column = dps * lax.rem(y + rows_y - s, rows_y) + d
        outs[s][...] = wide[pl.ds(column, inner, stride=rows_y * dps), :].astype(BF16)


def blocks(weights, rows_y, dps, after=()):
    num_cols, inner, here = weights.shape
    flat = weights.transpose(1, 0, 2).reshape(inner * num_cols, here)
    return pl.pallas_call(
        functools.partial(blocks_kernel, rows_y, dps),
        out_shape=[jax.ShapeDtypeStruct((inner, here), BF16)] * rows_y,
        in_specs=[VMEM] + [ANY] * len(after),
        out_specs=[VMEM] * rows_y,
        scratch_shapes=[pltpu.VMEM(flat.shape, F32)],
        compiler_params=params(16),
        name="blocks",
    )(flat, *after)


def filters_kernel(own, other, weight, turned):
    k = lax.rem(lax.axis_index("map"), CORES)
    for block, core in ((own[...], k), (other[...], 1 - k)):
        at = pl.multiple_of(core * LANES, LANES)
        weight[:, pl.ds(at, LANES)] = block
        turned[pl.ds(at, LANES), :] = block.T


def filters(own, other):
    inner, here = own.shape
    return pl.pallas_call(
        filters_kernel,
        out_shape=[
            jax.ShapeDtypeStruct((inner, CORES * here), BF16),
            jax.ShapeDtypeStruct((CORES * here, inner), BF16),
        ],
        in_specs=[VMEM] * 2,
        out_specs=[VMEM] * 2,
        compiler_params=params(8),
        name="filters",
    )(own, other)


def join_kernel(above, above_in, below, patch):
    mine = lax.rem(lax.axis_index("map"), CORES) == lax.axis_index("dp")

    @pl.when(mine)
    def _():
        patch[...] = above[...] + below[...]

    @pl.when(jnp.logical_not(mine))
    def _():
        patch[...] = above_in[...] + below[...]


def join(above, above_in, below):
    return pl.pallas_call(
        join_kernel,
        out_shape=jax.ShapeDtypeStruct(below.shape, BF16),
        in_specs=[VMEM] * 3,
        out_specs=VMEM,
        compiler_params=params(8),
        name="join",
    )(above, above_in, below)


def dot(a, b):
    return jnp.dot(a, b, preferred_element_type=F32)


def column_kernel(rows_y, patch_in, *refs):
    weight, turned = refs[:rows_y], refs[rows_y : 2 * rows_y]
    pe, mr, res, sq, inv = refs[2 * rows_y :]
    inner, count = patch_in.shape
    tile = weight[0].shape[1]
    maps = rows_y * tile
    pe[:, pl.ds(0, count)] = patch_in[...]
    patch = patch_in[...]
    for m in range(0, maps, tile):
        r = dot(turned[m // tile][...], patch)
        res[pl.ds(m, tile), :] = r
        mr[pl.ds(m, tile), pl.ds(count, count)] = r.astype(BF16)
        sq[pl.ds(m, tile), :] = r * r
    sq[pl.ds(maps, SUB), :] = sq[pl.ds(0, SUB), :]

    steps = -(-inner // tile)
    for n in range(steps):
        low, high = n * tile, min(inner, (n + 1) * tile)
        rows = pl.ds(low, high - low)
        error = -pe[rows, pl.ds(0, count)].astype(F32)
        for p in range(rows_y):
            error += dot(weight[p][rows, :], mr[pl.ds(p * tile, tile), pl.ds(count, count)])
        pe[rows, pl.ds(count, count)] = error.astype(BF16)
    for m in range(0, maps, tile):
        total = sq[pl.ds(m, tile), :]
        for i in range(1, POOL):
            total = total + sq[pl.ds(m + i, tile), :]
        inv[pl.ds(SUB + m, tile), :] = lax.rsqrt(smoothing + total)
    inv[pl.ds(0, SUB), :] = inv[pl.ds(maps, SUB), :]
    error_b = pe[:, pl.ds(count, count)]
    for m in range(0, maps, tile):
        back = dot(turned[m // tile][...], error_b)
        spread = inv[pl.ds(SUB + m, tile), :]
        for i in range(1, POOL):
            spread = spread + inv[pl.ds(SUB + m - i, tile), :]
        mixed = back + sparsity * res[pl.ds(m, tile), :] * spread
        mr[pl.ds(m, tile), pl.ds(0, count)] = mixed.astype(BF16)


def column(patch, weight, turned):
    inner, count = patch.shape
    rows_y = len(weight)
    maps = rows_y * weight[0].shape[1]
    return pl.pallas_call(
        functools.partial(column_kernel, rows_y),
        out_shape=[
            jax.ShapeDtypeStruct((inner, 2 * count), BF16),
            jax.ShapeDtypeStruct((maps, 2 * count), BF16),
        ],
        in_specs=[VMEM] * (1 + 2 * rows_y),
        out_specs=[VMEM] * 2,
        scratch_shapes=[
            pltpu.VMEM((maps, count), F32),
            pltpu.VMEM((maps + SUB, count), F32),
            pltpu.VMEM((maps + SUB, count), F32),
        ],
        compiler_params=params(40),
        name="column",
    )(patch, *weight, *turned)


def padded(rows):
    return -(-rows // 16) * 16


def piece_kernel(shifts, scale, pe, mr, *refs):
    home, away = refs[-2:]
    inner = pe.shape[0]
    first = lax.rem(lax.axis_index("map"), CORES) == 0
    tile = 256
    for i, p in enumerate(shifts):
        groups = mr[pl.ds(CORES * LANES * p, CORES * LANES), :]
        for n in range(0, inner, tile):
            size = min(tile, inner - n)
            g = lax.dot_general(
                pe[pl.ds(n, size), :], groups, (((1,), (1,)), ((), ())),
                preferred_element_type=F32,
            )
            g = g * scale
            low, high = g[:, :LANES], g[:, LANES:]
            rows = pl.ds(i * padded(inner) + n, size)
            home[rows, :] = jnp.where(first, low, high)
            away[rows, :] = jnp.where(first, high, low).astype(BF16)


def piece(shifts, pe, mr, after=()):
    inner, depth = pe.shape
    rows = len(shifts) * padded(inner)
    return pl.pallas_call(
        functools.partial(piece_kernel, shifts, 1.0 / depth),
        out_shape=[
            jax.ShapeDtypeStruct((rows, LANES), F32),
            jax.ShapeDtypeStruct((rows, LANES), BF16),
        ],
        in_specs=[VMEM] * 2 + [ANY] * len(after),
        out_specs=[VMEM] * 2,
        compiler_params=params(16),
        name="piece",
    )(pe, mr, *after)


def total_kernel(count, home, away, *refs):
    outs = refs[-count:]
    inner = outs[0].shape[0]
    for i, out in enumerate(outs):
        rows = pl.ds(i * padded(inner), inner)
        out[...] = (home[rows, :] + away[rows, :].astype(F32)).astype(BF16)


def total(home, away, count, inner, after):
    return pl.pallas_call(
        functools.partial(total_kernel, count),
        out_shape=[jax.ShapeDtypeStruct((inner, LANES), BF16)] * count,
        in_specs=[VMEM] * 2 + [ANY] * len(after),
        out_specs=[VMEM] * count,
        compiler_params=params(8),
        name="total",
    )(home, away, *after)


def follow_kernel(block, after, out):
    out[...] = block[...]


def follow(block, after):
    return pl.pallas_call(
        follow_kernel,
        out_shape=jax.ShapeDtypeStruct(block.shape, block.dtype),
        in_specs=[VMEM, ANY],
        out_specs=VMEM,
        compiler_params=params(4),
        name="follow",
    )(block, after)


def place_pieces(full, shifts, refs, rows_y, dps):
    y, d = lax.axis_index("map") // CORES, lax.axis_index("dp")
    inner = refs[0].shape[0]
    for n, s in enumerate(shifts):
        row = lax.rem(y + rows_y - s, rows_y)
        for block, part in ((refs[2 * n], d), (refs[2 * n + 1], 1 - d)):
            at = pl.ds(dps * row + part, inner, stride=rows_y * dps)
            full[at, :] = block[...].astype(F32)


def gather_kernel(rows_y, dps, shifts, *refs):
    place_pieces(refs[-1], shifts, refs[:-1], rows_y, dps)


def gather(pieces, shifts, rows_y, dps):
    inner, here = pieces[0].shape
    return pl.pallas_call(
        functools.partial(gather_kernel, rows_y, dps, shifts),
        out_shape=jax.ShapeDtypeStruct((inner * rows_y * dps, here), F32),
        in_specs=[VMEM] * len(pieces),
        out_specs=VMEM,
        compiler_params=params(8),
        name="gather",
    )(*pieces)


def finish_kernel(rows_y, dps, shifts, *refs):
    pieces, weights, early = refs[: 2 * len(shifts)], refs[-8], refs[-7]
    grad, fresh, full, new, grad_sem, sems = refs[-6:]
    full[...] = early[...]
    place_pieces(full, shifts, pieces, rows_y, dps)
    rows = full.shape[0]
    some = rows // dps
    at = pl.multiple_of(lax.axis_index("dp") * some, SUB)
    grad_copy = pltpu.make_async_copy(full.at[pl.ds(at, some), :], grad, grad_sem)
    grad_copy.start()
    copies = []
    for n, low in enumerate(range(0, rows, OUT_ROWS)):
        part = pl.ds(low, min(OUT_ROWS, rows - low))
        new[part, :] = (weights[part, :].astype(F32) - learn_rate * full[part, :]).astype(BF16)
        copy = pltpu.make_async_copy(new.at[part, :], fresh.at[part, :], sems.at[n])
        copy.start()
        copies.append(copy)
    grad_copy.wait()
    for copy in copies:
        copy.wait()


def finish(pieces, shifts, weights, full, rows_y, dps):
    num_cols, inner, here = weights.shape
    rows = inner * num_cols
    flat = weights.transpose(1, 0, 2).reshape(rows, here)
    grad, fresh = pl.pallas_call(
        functools.partial(finish_kernel, rows_y, dps, shifts),
        out_shape=[
            jax.ShapeDtypeStruct((rows // dps, here), F32),
            jax.ShapeDtypeStruct((rows, here), BF16),
        ],
        in_specs=[VMEM] * (len(pieces) + 2),
        out_specs=[HBM, HBM],
        scratch_shapes=[
            pltpu.VMEM((rows, here), F32),
            pltpu.VMEM((rows, here), BF16),
            pltpu.SemaphoreType.DMA,
            pltpu.SemaphoreType.DMA((-(-rows // OUT_ROWS),)),
        ],
        compiler_params=params(16),
        name="finish",
    )(*pieces, flat, full)
    grad = grad.reshape(inner // dps, num_cols, here).transpose(1, 0, 2)
    return grad, fresh.reshape(inner, num_cols, here).transpose(1, 0, 2)


def per_device(mesh_shape, frames, weights, offsets):
    rows_y = mesh_shape[1] // CORES
    def send(x, move):
        return lax.ppermute(x, AXES, table(mesh_shape, move))

    dps = mesh_shape[2]
    places = offsets.T
    upper = send(places, lambda t, y, k, d: (t + 1, y, k, d))
    own = blocks(weights, rows_y, dps)
    below, token = cut(frames, upper, False, (own[0],))
    below = send(below, lambda t, y, k, d: (t - 1, y, d, k))

    own = [own[0]] + [
        send(own[s], lambda t, y, k, d: (t, y - s, k, d)) for s in range(1, rows_y)
    ]
    above, _ = cut(frames, places, True, own[1:])
    weight, turned = [], []
    for block in own:
        pair = filters(block, send(block, lambda t, y, k, d: (t, y, 1 - k, d)))
        weight.append(pair[0])
        turned.append(pair[1])
    above_in = send(above, lambda t, y, k, d: (t, y, d, k) if k != d else None)
    above_in = send(above, lambda t, y, k, d: (t, y, d, k) if k != d else None)

    pe, mr = column(join(above, above_in, below), weight, turned)

    pieces = {}
    inner = weights.shape[1]
    after_piece, after_total = (), ()
    for shifts in ((0,), (1, 3, 2)):
        home, away = piece(shifts, pe, mr, after_piece)
        after_piece = (away,)
        away = send(away, lambda t, y, k, d: (t, y, 1 - k, d))
        blocks_here = total(home, away, len(shifts), inner, after_total)
        after_total = (blocks_here[0],)
        for s, block in zip(shifts, blocks_here):
            if s == 2:
                block = follow(block, pieces[0][1])
            if s:
                block = send(block, lambda t, y, k, d: (t, y + s, k, d))
            pieces[s] = [block, send(block, lambda t, y, k, d: (t, y, k, 1 - d))]
    early, late = (0, 1, 3), (2,)
    full = gather(sum([pieces[s] for s in early], []), early, rows_y, dps)
    return finish(sum([pieces[s] for s in late], []), late, weights, full, rows_y, dps)


def solution(mesh):
    mesh_shape = tuple(mesh.shape[a] for a in AXES)
    placed = (P(None, "tile", None, "dp"), P("tile", None, "map"), P("tile", None))

    def run(frames, weights, offsets):
        return per_device(mesh_shape, frames, weights, offsets)

    return jax.shard_map(
        run,
        mesh=mesh,
        in_specs=placed,
        out_specs=(P("tile", "dp", "map"), P("tile", None, "map")),
        check_vma=False,
    )
```

```python
import functools

import jax
import jax.numpy as jnp
from jax import lax
from jax.experimental import pallas as pl
from jax.experimental.pallas import tpu as pltpu
from jax.sharding import PartitionSpec as P

FIELD = 18
POOL = 5
CORES = 2
STRIP = 48
SUB = 8
LANES = 128
MIB = 1 << 20
CUT_MIB = 50
OUT_ROWS = 2048

smoothing = 1.0
sparsity = 3.0
learn_rate = 0.1

AXES = ("tile", "map", "dp")
F32, BF16 = jnp.float32, jnp.bfloat16
VMEM = pl.BlockSpec(memory_space=pltpu.VMEM)
SMEM = pl.BlockSpec(memory_space=pltpu.SMEM)
ANY = pl.BlockSpec(memory_space=pl.ANY)
HBM = pl.BlockSpec(memory_space=pltpu.HBM)


def table(mesh_shape, move):
    tiles, maps, dps = mesh_shape
    rows_y = maps // CORES
    pairs = []
    for t in range(tiles):
        for y in range(rows_y):
            for k in range(CORES):
                for d in range(dps):
                    to = move(t, y, k, d)
                    if to is None or not 0 <= to[0] < tiles:
                        continue
                    t2, y2, k2, d2 = to
                    source = (t * maps + y * CORES + k) * dps + d
                    target = (t2 * maps + (y2 % rows_y) * CORES + k2) * dps + d2
                    pairs.append((source, target))
    return pairs


def params(mib):
    return pltpu.CompilerParams(vmem_limit_bytes=mib * MIB)


def cut_kernel(above, places, frames, *refs):
    out, token, strip, wide, flat, sems = refs[-6:]
    channels, rows_here, across, count = frames.shape
    column = lax.axis_index("map")
    top, left = places[0, column], places[1, column]
    base = jnp.minimum(left // 16 * 16, across - STRIP)
    base = pl.multiple_of(base, 16)
    first = jnp.minimum(top, rows_here - FIELD) if above else 0
    copies = [
        pltpu.make_async_copy(
            frames.at[channel, pl.ds(first, FIELD), pl.ds(base, STRIP), :],
            strip.at[channel],
            sems.at[channel],
        )
        for channel in range(channels)
    ]
    for copy in copies:
        copy.start()
    token[...] = jnp.zeros_like(token)
    shift = left - base
    for channel in range(channels):
        copies[channel].wait()
        for n in range(count // LANES):
            lanes = strip[channel, :, :, pl.ds(n * LANES, LANES)]
            wide[n] = lanes.reshape(FIELD * STRIP, LANES).astype(F32)
        for r in range(FIELD):
            row = top + r - (first if above else rows_here)
            valid = (row < FIELD) if above else (row >= 0)
            row = jnp.clip(row, 0, FIELD - 1)
            for n in range(count // LANES):
                x = wide[n, pl.ds(row * STRIP + shift, FIELD), :]
                x = jnp.where(valid, x, 0.0)
                at = pl.ds((channel * FIELD + r) * FIELD, FIELD)
                flat[at, pl.ds(n * LANES, LANES)] = x
    inner = channels * FIELD * FIELD
    out[...] = flat[pl.ds(0, inner), :].astype(BF16)


def cut(frames, places, above, after=()):
    channels, rows_here, wide, count = frames.shape
    inner = channels * FIELD * FIELD
    return pl.pallas_call(
        functools.partial(cut_kernel, above),
        out_shape=[
            jax.ShapeDtypeStruct((inner, count), BF16),
            jax.ShapeDtypeStruct((SUB, LANES), F32),
        ],
        in_specs=[SMEM, HBM] + [ANY] * len(after),
        out_specs=[VMEM] * 2,
        scratch_shapes=[
            pltpu.VMEM((channels, FIELD, STRIP, count), BF16),
            pltpu.VMEM((count // LANES, FIELD * STRIP, LANES), F32),
            pltpu.VMEM((inner, count), F32),
            pltpu.SemaphoreType.DMA((channels,)),
        ],
        compiler_params=params(CUT_MIB),
        name="cut_above" if above else "cut_below",
    )(places, frames, *after)


def blocks_kernel(rows_y, dps, flat, *refs):
    outs, wide = refs[-1 - rows_y : -1], refs[-1]
    inner = outs[0].shape[0]
    y, d = lax.axis_index("map") // CORES, lax.axis_index("dp")
    wide[...] = flat[...].astype(F32)
    for s in range(rows_y):
        column = dps * lax.rem(y + rows_y - s, rows_y) + d
        outs[s][...] = wide[pl.ds(column, inner, stride=rows_y * dps), :].astype(BF16)


def blocks(weights, rows_y, dps, after=()):
    num_cols, inner, here = weights.shape
    flat = weights.transpose(1, 0, 2).reshape(inner * num_cols, here)
    return pl.pallas_call(
        functools.partial(blocks_kernel, rows_y, dps),
        out_shape=[jax.ShapeDtypeStruct((inner, here), BF16)] * rows_y,
        in_specs=[VMEM] + [ANY] * len(after),
        out_specs=[VMEM] * rows_y,
        scratch_shapes=[pltpu.VMEM(flat.shape, F32)],
        compiler_params=params(16),
        name="blocks",
    )(flat, *after)


def filters_kernel(own, other, weight, turned):
    k = lax.rem(lax.axis_index("map"), CORES)
    for block, core in ((own[...], k), (other[...], 1 - k)):
        at = pl.multiple_of(core * LANES, LANES)
        weight[:, pl.ds(at, LANES)] = block
        turned[pl.ds(at, LANES), :] = block.T


def filters(own, other):
    inner, here = own.shape
    return pl.pallas_call(
        filters_kernel,
        out_shape=[
            jax.ShapeDtypeStruct((inner, CORES * here), BF16),
            jax.ShapeDtypeStruct((CORES * here, inner), BF16),
        ],
        in_specs=[VMEM] * 2,
        out_specs=[VMEM] * 2,
        compiler_params=params(8),
        name="filters",
    )(own, other)


def join_kernel(above, above_in, below, patch):
    mine = lax.rem(lax.axis_index("map"), CORES) == lax.axis_index("dp")

    @pl.when(mine)
    def _():
        patch[...] = above[...] + below[...]

    @pl.when(jnp.logical_not(mine))
    def _():
        patch[...] = above_in[...] + below[...]


def join(above, above_in, below):
    return pl.pallas_call(
        join_kernel,
        out_shape=jax.ShapeDtypeStruct(below.shape, BF16),
        in_specs=[VMEM] * 3,
        out_specs=VMEM,
        compiler_params=params(8),
        name="join",
    )(above, above_in, below)


def dot(a, b):
    return jnp.dot(a, b, preferred_element_type=F32)


def column_kernel(rows_y, patch_in, *refs):
    weight, turned = refs[:rows_y], refs[rows_y : 2 * rows_y]
    pe, mr, res, sq, inv = refs[2 * rows_y :]
    inner, count = patch_in.shape
    tile = weight[0].shape[1]
    maps = rows_y * tile
    pe[:, pl.ds(0, count)] = patch_in[...]
    patch = patch_in[...]
    for m in range(0, maps, tile):
        r = dot(turned[m // tile][...], patch)
        res[pl.ds(m, tile), :] = r
        mr[pl.ds(m, tile), pl.ds(count, count)] = r.astype(BF16)
        sq[pl.ds(m, tile), :] = r * r
    sq[pl.ds(maps, SUB), :] = sq[pl.ds(0, SUB), :]

    steps = -(-inner // tile)
    for n in range(steps):
        low, high = n * tile, min(inner, (n + 1) * tile)
        rows = pl.ds(low, high - low)
        error = -pe[rows, pl.ds(0, count)].astype(F32)
        for p in range(rows_y):
            error += dot(weight[p][rows, :], mr[pl.ds(p * tile, tile), pl.ds(count, count)])
        pe[rows, pl.ds(count, count)] = error.astype(BF16)
    for m in range(0, maps, tile):
        total = sq[pl.ds(m, tile), :]
        for i in range(1, POOL):
            total = total + sq[pl.ds(m + i, tile), :]
        inv[pl.ds(SUB + m, tile), :] = lax.rsqrt(smoothing + total)
    inv[pl.ds(0, SUB), :] = inv[pl.ds(maps, SUB), :]
    error_b = pe[:, pl.ds(count, count)]
    for m in range(0, maps, tile):
        back = dot(turned[m // tile][...], error_b)
        spread = inv[pl.ds(SUB + m, tile), :]
        for i in range(1, POOL):
            spread = spread + inv[pl.ds(SUB + m - i, tile), :]
        mixed = back + sparsity * res[pl.ds(m, tile), :] * spread
        mr[pl.ds(m, tile), pl.ds(0, count)] = mixed.astype(BF16)


def column(patch, weight, turned):
    inner, count = patch.shape
    rows_y = len(weight)
    maps = rows_y * weight[0].shape[1]
    return pl.pallas_call(
        functools.partial(column_kernel, rows_y),
        out_shape=[
            jax.ShapeDtypeStruct((inner, 2 * count), BF16),
            jax.ShapeDtypeStruct((maps, 2 * count), BF16),
        ],
        in_specs=[VMEM] * (1 + 2 * rows_y),
        out_specs=[VMEM] * 2,
        scratch_shapes=[
            pltpu.VMEM((maps, count), F32),
            pltpu.VMEM((maps + SUB, count), F32),
            pltpu.VMEM((maps + SUB, count), F32),
        ],
        compiler_params=params(40),
        name="column",
    )(patch, *weight, *turned)


def padded(rows):
    return -(-rows // 16) * 16


def piece_kernel(shifts, scale, pe, mr, *refs):
    home, away = refs[-2:]
    inner = pe.shape[0]
    first = lax.rem(lax.axis_index("map"), CORES) == 0
    tile = 256
    for i, p in enumerate(shifts):
        groups = mr[pl.ds(CORES * LANES * p, CORES * LANES), :]
        for n in range(0, inner, tile):
            size = min(tile, inner - n)
            g = lax.dot_general(
                pe[pl.ds(n, size), :], groups, (((1,), (1,)), ((), ())),
                preferred_element_type=F32,
            )
            g = g * scale
            low, high = g[:, :LANES], g[:, LANES:]
            rows = pl.ds(i * padded(inner) + n, size)
            home[rows, :] = jnp.where(first, low, high)
            away[rows, :] = jnp.where(first, high, low).astype(BF16)


def piece(shifts, pe, mr, after=()):
    inner, depth = pe.shape
    rows = len(shifts) * padded(inner)
    return pl.pallas_call(
        functools.partial(piece_kernel, shifts, 1.0 / depth),
        out_shape=[
            jax.ShapeDtypeStruct((rows, LANES), F32),
            jax.ShapeDtypeStruct((rows, LANES), BF16),
        ],
        in_specs=[VMEM] * 2 + [ANY] * len(after),
        out_specs=[VMEM] * 2,
        compiler_params=params(16),
        name="piece",
    )(pe, mr, *after)


def total_kernel(count, home, away, *refs):
    outs = refs[-count:]
    inner = outs[0].shape[0]
    for i, out in enumerate(outs):
        rows = pl.ds(i * padded(inner), inner)
        out[...] = (home[rows, :] + away[rows, :].astype(F32)).astype(BF16)


def total(home, away, count, inner, after):
    return pl.pallas_call(
        functools.partial(total_kernel, count),
        out_shape=[jax.ShapeDtypeStruct((inner, LANES), BF16)] * count,
        in_specs=[VMEM] * 2 + [ANY] * len(after),
        out_specs=[VMEM] * count,
        compiler_params=params(8),
        name="total",
    )(home, away, *after)


def follow_kernel(block, after, out):
    out[...] = block[...]


def follow(block, after):
    return pl.pallas_call(
        follow_kernel,
        out_shape=jax.ShapeDtypeStruct(block.shape, block.dtype),
        in_specs=[VMEM, ANY],
        out_specs=VMEM,
        compiler_params=params(4),
        name="follow",
    )(block, after)


def place_pieces(full, shifts, refs, rows_y, dps):
    y, d = lax.axis_index("map") // CORES, lax.axis_index("dp")
    inner = refs[0].shape[0]
    for n, s in enumerate(shifts):
        row = lax.rem(y + rows_y - s, rows_y)
        for block, part in ((refs[2 * n], d), (refs[2 * n + 1], 1 - d)):
            at = pl.ds(dps * row + part, inner, stride=rows_y * dps)
            full[at, :] = block[...].astype(F32)


def gather_kernel(rows_y, dps, shifts, *refs):
    place_pieces(refs[-1], shifts, refs[:-1], rows_y, dps)


def gather(pieces, shifts, rows_y, dps):
    inner, here = pieces[0].shape
    return pl.pallas_call(
        functools.partial(gather_kernel, rows_y, dps, shifts),
        out_shape=jax.ShapeDtypeStruct((inner * rows_y * dps, here), F32),
        in_specs=[VMEM] * len(pieces),
        out_specs=VMEM,
        compiler_params=params(8),
        name="gather",
    )(*pieces)


def finish_kernel(rows_y, dps, shifts, *refs):
    pieces, weights, early = refs[: 2 * len(shifts)], refs[-8], refs[-7]
    grad, fresh, full, new, grad_sem, sems = refs[-6:]
    full[...] = early[...]
    place_pieces(full, shifts, pieces, rows_y, dps)
    rows = full.shape[0]
    some = rows // dps
    at = pl.multiple_of(lax.axis_index("dp") * some, SUB)
    grad_copy = pltpu.make_async_copy(full.at[pl.ds(at, some), :], grad, grad_sem)
    grad_copy.start()
    copies = []
    for n, low in enumerate(range(0, rows, OUT_ROWS)):
        part = pl.ds(low, min(OUT_ROWS, rows - low))
        new[part, :] = (weights[part, :].astype(F32) - learn_rate * full[part, :]).astype(BF16)
        copy = pltpu.make_async_copy(new.at[part, :], fresh.at[part, :], sems.at[n])
        copy.start()
        copies.append(copy)
    grad_copy.wait()
    for copy in copies:
        copy.wait()


def finish(pieces, shifts, weights, full, rows_y, dps):
    num_cols, inner, here = weights.shape
    rows = inner * num_cols
    flat = weights.transpose(1, 0, 2).reshape(rows, here)
    grad, fresh = pl.pallas_call(
        functools.partial(finish_kernel, rows_y, dps, shifts),
        out_shape=[
            jax.ShapeDtypeStruct((rows // dps, here), F32),
            jax.ShapeDtypeStruct((rows, here), BF16),
        ],
        in_specs=[VMEM] * (len(pieces) + 2),
        out_specs=[HBM, HBM],
        scratch_shapes=[
            pltpu.VMEM((rows, here), F32),
            pltpu.VMEM((rows, here), BF16),
            pltpu.SemaphoreType.DMA,
            pltpu.SemaphoreType.DMA((-(-rows // OUT_ROWS),)),
        ],
        compiler_params=params(16),
        name="finish",
    )(*pieces, flat, full)
    grad = grad.reshape(inner // dps, num_cols, here).transpose(1, 0, 2)
    return grad, fresh.reshape(inner, num_cols, here).transpose(1, 0, 2)


def per_device(mesh_shape, frames, weights, offsets):
    rows_y = mesh_shape[1] // CORES
    def send(x, move):
        return lax.ppermute(x, AXES, table(mesh_shape, move))

    dps = mesh_shape[2]
    places = offsets.T
    upper = send(places, lambda t, y, k, d: (t + 1, y, k, d))
    own = blocks(weights, rows_y, dps)
    above, token = cut(frames, places, True)
    below, token = cut(frames, upper, False, (token,))
    below = send(below, lambda t, y, k, d: (t - 1, y, d, k))

    weight, turned = [], []
    for s in range(rows_y):
        block = own[s]
        if s:
            block = send(block, lambda t, y, k, d: (t, y - s, k, d))
        other = send(block, lambda t, y, k, d: (t, y, 1 - k, d))
        pair = filters(block, other)
        weight.append(pair[0])
        turned.append(pair[1])
    above_in = send(above, lambda t, y, k, d: (t, y, d, k) if k != d else None)

    pe, mr = column(join(above, above_in, below), weight, turned)

    pieces = {}
    inner = weights.shape[1]
    after_piece, after_total = (), ()
    for shifts in ((0,), (1, 3, 2)):
        home, away = piece(shifts, pe, mr, after_piece)
        after_piece = (away,)
        away = send(away, lambda t, y, k, d: (t, y, 1 - k, d))
        blocks_here = total(home, away, len(shifts), inner, after_total)
        after_total = (blocks_here[0],)
        for s, block in zip(shifts, blocks_here):
            if s == 2:
                block = follow(block, pieces[0][1])
            if s:
                block = send(block, lambda t, y, k, d: (t, y + s, k, d))
            pieces[s] = [block, send(block, lambda t, y, k, d: (t, y, k, 1 - d))]
    early, late = (0, 1, 3), (2,)
    full = gather(sum([pieces[s] for s in early], []), early, rows_y, dps)
    return finish(sum([pieces[s] for s in late], []), late, weights, full, rows_y, dps)


def solution(mesh):
    mesh_shape = tuple(mesh.shape[a] for a in AXES)
    placed = (P(None, "tile", None, "dp"), P("tile", None, "map"), P("tile", None))

    def run(frames, weights, offsets):
        return per_device(mesh_shape, frames, weights, offsets)

    return jax.shard_map(
        run,
        mesh=mesh,
        in_specs=placed,
        out_specs=(P("tile", "dp", "map"), P("tile", None, "map")),
        check_vma=False,
    )
```

```python
import functools

import jax
import jax.numpy as jnp
from jax import lax
from jax.experimental import pallas as pl
from jax.experimental.pallas import tpu as pltpu
from jax.sharding import PartitionSpec as P

FIELD = 18
POOL = 5
CORES = 2
STRIP = 48
SUB = 8
LANES = 128
MIB = 1 << 20
CUT_MIB = 50
OUT_ROWS = 2048

smoothing = 1.0
sparsity = 3.0
learn_rate = 0.1

AXES = ("tile", "map", "dp")
F32, BF16 = jnp.float32, jnp.bfloat16
VMEM = pl.BlockSpec(memory_space=pltpu.VMEM)
SMEM = pl.BlockSpec(memory_space=pltpu.SMEM)
ANY = pl.BlockSpec(memory_space=pl.ANY)
HBM = pl.BlockSpec(memory_space=pltpu.HBM)


def table(mesh_shape, move):
    tiles, maps, dps = mesh_shape
    rows_y = maps // CORES
    pairs = []
    for t in range(tiles):
        for y in range(rows_y):
            for k in range(CORES):
                for d in range(dps):
                    to = move(t, y, k, d)
                    if to is None or not 0 <= to[0] < tiles:
                        continue
                    t2, y2, k2, d2 = to
                    source = (t * maps + y * CORES + k) * dps + d
                    target = (t2 * maps + (y2 % rows_y) * CORES + k2) * dps + d2
                    pairs.append((source, target))
    return pairs


def params(mib):
    return pltpu.CompilerParams(vmem_limit_bytes=mib * MIB)


def cut_kernel(above, places, frames, *refs):
    out, token, strip, wide, flat, sems = refs[-6:]
    channels, rows_here, across, count = frames.shape
    column = lax.axis_index("map")
    top, left = places[0, column], places[1, column]
    base = jnp.minimum(left // 16 * 16, across - STRIP)
    base = pl.multiple_of(base, 16)
    first = jnp.minimum(top, rows_here - FIELD) if above else 0
    copies = [
        pltpu.make_async_copy(
            frames.at[channel, pl.ds(first, FIELD), pl.ds(base, STRIP), :],
            strip.at[channel],
            sems.at[channel],
        )
        for channel in range(channels)
    ]
    for copy in copies:
        copy.start()
    token[...] = jnp.zeros_like(token)
    shift = left - base
    for channel in range(channels):
        copies[channel].wait()
        for n in range(count // LANES):
            lanes = strip[channel, :, :, pl.ds(n * LANES, LANES)]
            wide[n] = lanes.reshape(FIELD * STRIP, LANES).astype(F32)
        for r in range(FIELD):
            row = top + r - (first if above else rows_here)
            valid = (row < FIELD) if above else (row >= 0)
            row = jnp.clip(row, 0, FIELD - 1)
            for n in range(count // LANES):
                x = wide[n, pl.ds(row * STRIP + shift, FIELD), :]
                x = jnp.where(valid, x, 0.0)
                at = pl.ds((channel * FIELD + r) * FIELD, FIELD)
                flat[at, pl.ds(n * LANES, LANES)] = x
    inner = channels * FIELD * FIELD
    out[...] = flat[pl.ds(0, inner), :].astype(BF16)


def cut(frames, places, above, after=()):
    channels, rows_here, wide, count = frames.shape
    inner = channels * FIELD * FIELD
    return pl.pallas_call(
        functools.partial(cut_kernel, above),
        out_shape=[
            jax.ShapeDtypeStruct((inner, count), BF16),
            jax.ShapeDtypeStruct((SUB, LANES), F32),
        ],
        in_specs=[SMEM, HBM] + [ANY] * len(after),
        out_specs=[VMEM] * 2,
        scratch_shapes=[
            pltpu.VMEM((channels, FIELD, STRIP, count), BF16),
            pltpu.VMEM((count // LANES, FIELD * STRIP, LANES), F32),
            pltpu.VMEM((inner, count), F32),
            pltpu.SemaphoreType.DMA((channels,)),
        ],
        compiler_params=params(CUT_MIB),
        name="cut_above" if above else "cut_below",
    )(places, frames, *after)


def blocks_kernel(rows_y, dps, flat, *refs):
    outs, wide = refs[-1 - rows_y : -1], refs[-1]
    inner = outs[0].shape[0]
    y, d = lax.axis_index("map") // CORES, lax.axis_index("dp")
    wide[...] = flat[...].astype(F32)
    for s in range(rows_y):
        column = dps * lax.rem(y + rows_y - s, rows_y) + d
        outs[s][...] = wide[pl.ds(column, inner, stride=rows_y * dps), :].astype(BF16)


def blocks(weights, rows_y, dps, after=()):
    num_cols, inner, here = weights.shape
    flat = weights.transpose(1, 0, 2).reshape(inner * num_cols, here)
    return pl.pallas_call(
        functools.partial(blocks_kernel, rows_y, dps),
        out_shape=[jax.ShapeDtypeStruct((inner, here), BF16)] * rows_y,
        in_specs=[VMEM] + [ANY] * len(after),
        out_specs=[VMEM] * rows_y,
        scratch_shapes=[pltpu.VMEM(flat.shape, F32)],
        compiler_params=params(16),
        name="blocks",
    )(flat, *after)


def filters_kernel(own, other, weight, turned):
    k = lax.rem(lax.axis_index("map"), CORES)
    for block, core in ((own[...], k), (other[...], 1 - k)):
        at = pl.multiple_of(core * LANES, LANES)
        weight[:, pl.ds(at, LANES)] = block
        turned[pl.ds(at, LANES), :] = block.T


def filters(own, other):
    inner, here = own.shape
    return pl.pallas_call(
        filters_kernel,
        out_shape=[
            jax.ShapeDtypeStruct((inner, CORES * here), BF16),
            jax.ShapeDtypeStruct((CORES * here, inner), BF16),
        ],
        in_specs=[VMEM] * 2,
        out_specs=[VMEM] * 2,
        compiler_params=params(8),
        name="filters",
    )(own, other)


def join_kernel(above, above_in, below, patch):
    mine = lax.rem(lax.axis_index("map"), CORES) == lax.axis_index("dp")

    @pl.when(mine)
    def _():
        patch[...] = above[...] + below[...]

    @pl.when(jnp.logical_not(mine))
    def _():
        patch[...] = above_in[...] + below[...]


def join(above, above_in, below):
    return pl.pallas_call(
        join_kernel,
        out_shape=jax.ShapeDtypeStruct(below.shape, BF16),
        in_specs=[VMEM] * 3,
        out_specs=VMEM,
        compiler_params=params(8),
        name="join",
    )(above, above_in, below)


def dot(a, b):
    return jnp.dot(a, b, preferred_element_type=F32)


def column_kernel(rows_y, patch_in, *refs):
    weight, turned = refs[:rows_y], refs[rows_y : 2 * rows_y]
    pe, mr, res, sq, inv = refs[2 * rows_y :]
    inner, count = patch_in.shape
    tile = weight[0].shape[1]
    maps = rows_y * tile
    pe[:, pl.ds(0, count)] = patch_in[...]
    patch = patch_in[...]
    for m in range(0, maps, tile):
        r = dot(turned[m // tile][...], patch)
        res[pl.ds(m, tile), :] = r
        mr[pl.ds(m, tile), pl.ds(count, count)] = r.astype(BF16)
        sq[pl.ds(m, tile), :] = r * r
    sq[pl.ds(maps, SUB), :] = sq[pl.ds(0, SUB), :]

    steps = -(-inner // tile)
    for n in range(steps):
        low, high = n * tile, min(inner, (n + 1) * tile)
        rows = pl.ds(low, high - low)
        error = -pe[rows, pl.ds(0, count)].astype(F32)
        for p in range(rows_y):
            error += dot(weight[p][rows, :], mr[pl.ds(p * tile, tile), pl.ds(count, count)])
        pe[rows, pl.ds(count, count)] = error.astype(BF16)
    for m in range(0, maps, tile):
        total = sq[pl.ds(m, tile), :]
        for i in range(1, POOL):
            total = total + sq[pl.ds(m + i, tile), :]
        inv[pl.ds(SUB + m, tile), :] = lax.rsqrt(smoothing + total)
    inv[pl.ds(0, SUB), :] = inv[pl.ds(maps, SUB), :]
    error_b = pe[:, pl.ds(count, count)]
    for m in range(0, maps, tile):
        back = dot(turned[m // tile][...], error_b)
        spread = inv[pl.ds(SUB + m, tile), :]
        for i in range(1, POOL):
            spread = spread + inv[pl.ds(SUB + m - i, tile), :]
        mixed = back + sparsity * res[pl.ds(m, tile), :] * spread
        mr[pl.ds(m, tile), pl.ds(0, count)] = mixed.astype(BF16)


def column(patch, weight, turned):
    inner, count = patch.shape
    rows_y = len(weight)
    maps = rows_y * weight[0].shape[1]
    return pl.pallas_call(
        functools.partial(column_kernel, rows_y),
        out_shape=[
            jax.ShapeDtypeStruct((inner, 2 * count), BF16),
            jax.ShapeDtypeStruct((maps, 2 * count), BF16),
        ],
        in_specs=[VMEM] * (1 + 2 * rows_y),
        out_specs=[VMEM] * 2,
        scratch_shapes=[
            pltpu.VMEM((maps, count), F32),
            pltpu.VMEM((maps + SUB, count), F32),
            pltpu.VMEM((maps + SUB, count), F32),
        ],
        compiler_params=params(40),
        name="column",
    )(patch, *weight, *turned)


def padded(rows):
    return -(-rows // 16) * 16


def piece_kernel(shifts, scale, pe, mr, *refs):
    home, away = refs[-2:]
    inner = pe.shape[0]
    first = lax.rem(lax.axis_index("map"), CORES) == 0
    tile = 256
    for i, p in enumerate(shifts):
        groups = mr[pl.ds(CORES * LANES * p, CORES * LANES), :]
        for n in range(0, inner, tile):
            size = min(tile, inner - n)
            g = lax.dot_general(
                pe[pl.ds(n, size), :], groups, (((1,), (1,)), ((), ())),
                preferred_element_type=F32,
            )
            g = g * scale
            low, high = g[:, :LANES], g[:, LANES:]
            rows = pl.ds(i * padded(inner) + n, size)
            home[rows, :] = jnp.where(first, low, high)
            away[rows, :] = jnp.where(first, high, low).astype(BF16)


def piece(shifts, pe, mr, after=()):
    inner, depth = pe.shape
    rows = len(shifts) * padded(inner)
    return pl.pallas_call(
        functools.partial(piece_kernel, shifts, 1.0 / depth),
        out_shape=[
            jax.ShapeDtypeStruct((rows, LANES), F32),
            jax.ShapeDtypeStruct((rows, LANES), BF16),
        ],
        in_specs=[VMEM] * 2 + [ANY] * len(after),
        out_specs=[VMEM] * 2,
        compiler_params=params(16),
        name="piece",
    )(pe, mr, *after)


def total_kernel(count, home, away, *refs):
    outs = refs[-count:]
    inner = outs[0].shape[0]
    for i, out in enumerate(outs):
        rows = pl.ds(i * padded(inner), inner)
        out[...] = (home[rows, :] + away[rows, :].astype(F32)).astype(BF16)


def total(home, away, count, inner, after):
    return pl.pallas_call(
        functools.partial(total_kernel, count),
        out_shape=[jax.ShapeDtypeStruct((inner, LANES), BF16)] * count,
        in_specs=[VMEM] * 2 + [ANY] * len(after),
        out_specs=[VMEM] * count,
        compiler_params=params(8),
        name="total",
    )(home, away, *after)


def follow_kernel(block, after, out):
    out[...] = block[...]


def follow(block, after):
    return pl.pallas_call(
        follow_kernel,
        out_shape=jax.ShapeDtypeStruct(block.shape, block.dtype),
        in_specs=[VMEM, ANY],
        out_specs=VMEM,
        compiler_params=params(4),
        name="follow",
    )(block, after)


def place_pieces(full, shifts, refs, rows_y, dps):
    y, d = lax.axis_index("map") // CORES, lax.axis_index("dp")
    inner = refs[0].shape[0]
    for n, s in enumerate(shifts):
        row = lax.rem(y + rows_y - s, rows_y)
        for block, part in ((refs[2 * n], d), (refs[2 * n + 1], 1 - d)):
            at = pl.ds(dps * row + part, inner, stride=rows_y * dps)
            full[at, :] = block[...].astype(F32)


def gather_kernel(rows_y, dps, shifts, *refs):
    place_pieces(refs[-1], shifts, refs[:-1], rows_y, dps)


def gather(pieces, shifts, rows_y, dps):
    inner, here = pieces[0].shape
    return pl.pallas_call(
        functools.partial(gather_kernel, rows_y, dps, shifts),
        out_shape=jax.ShapeDtypeStruct((inner * rows_y * dps, here), F32),
        in_specs=[VMEM] * len(pieces),
        out_specs=VMEM,
        compiler_params=params(8),
        name="gather",
    )(*pieces)


def finish_kernel(rows_y, dps, shifts, *refs):
    pieces, weights, early = refs[: 2 * len(shifts)], refs[-8], refs[-7]
    grad, fresh, full, new, grad_sem, sems = refs[-6:]
    full[...] = early[...]
    place_pieces(full, shifts, pieces, rows_y, dps)
    rows = full.shape[0]
    some = rows // dps
    at = pl.multiple_of(lax.axis_index("dp") * some, SUB)
    grad_copy = pltpu.make_async_copy(full.at[pl.ds(at, some), :], grad, grad_sem)
    grad_copy.start()
    copies = []
    for n, low in enumerate(range(0, rows, OUT_ROWS)):
        part = pl.ds(low, min(OUT_ROWS, rows - low))
        new[part, :] = (weights[part, :].astype(F32) - learn_rate * full[part, :]).astype(BF16)
        copy = pltpu.make_async_copy(new.at[part, :], fresh.at[part, :], sems.at[n])
        copy.start()
        copies.append(copy)
    grad_copy.wait()
    for copy in copies:
        copy.wait()


def finish(pieces, shifts, weights, full, rows_y, dps):
    num_cols, inner, here = weights.shape
    rows = inner * num_cols
    flat = weights.transpose(1, 0, 2).reshape(rows, here)
    grad, fresh = pl.pallas_call(
        functools.partial(finish_kernel, rows_y, dps, shifts),
        out_shape=[
            jax.ShapeDtypeStruct((rows // dps, here), F32),
            jax.ShapeDtypeStruct((rows, here), BF16),
        ],
        in_specs=[VMEM] * (len(pieces) + 2),
        out_specs=[HBM, HBM],
        scratch_shapes=[
            pltpu.VMEM((rows, here), F32),
            pltpu.VMEM((rows, here), BF16),
            pltpu.SemaphoreType.DMA,
            pltpu.SemaphoreType.DMA((-(-rows // OUT_ROWS),)),
        ],
        compiler_params=params(16),
        name="finish",
    )(*pieces, flat, full)
    grad = grad.reshape(inner // dps, num_cols, here).transpose(1, 0, 2)
    return grad, fresh.reshape(inner, num_cols, here).transpose(1, 0, 2)


def per_device(mesh_shape, frames, weights, offsets):
    rows_y = mesh_shape[1] // CORES
    def send(x, move):
        return lax.ppermute(x, AXES, table(mesh_shape, move))

    dps = mesh_shape[2]
    places = offsets.T
    upper = send(places, lambda t, y, k, d: (t + 1, y, k, d))
    above, token = cut(frames, places, True)
    below, token = cut(frames, upper, False, (token,))
    own = blocks(weights, rows_y, dps, (token,))
    below = send(below, lambda t, y, k, d: (t - 1, y, d, k))

    weight, turned = [], []
    for s in range(rows_y):
        block = own[s]
        if s:
            block = send(block, lambda t, y, k, d: (t, y - s, k, d))
        other = send(block, lambda t, y, k, d: (t, y, 1 - k, d))
        pair = filters(block, other)
        weight.append(pair[0])
        turned.append(pair[1])
    above_in = send(above, lambda t, y, k, d: (t, y, d, k) if k != d else None)

    pe, mr = column(join(above, above_in, below), weight, turned)

    pieces = {}
    inner = weights.shape[1]
    for s in (0, 1, 3, 2):
        home, away = piece((s,), pe, mr)
        away = send(away, lambda t, y, k, d: (t, y, 1 - k, d))
        (block,) = total(home, away, 1, inner, ())
        if s == 2:
            block = follow(block, pieces[0][1])
        if s:
            block = send(block, lambda t, y, k, d: (t, y + s, k, d))
        pieces[s] = [block, send(block, lambda t, y, k, d: (t, y, k, 1 - d))]
    early, late = (0, 1, 3), (2,)
    full = gather(sum([pieces[s] for s in early], []), early, rows_y, dps)
    return finish(sum([pieces[s] for s in late], []), late, weights, full, rows_y, dps)


def solution(mesh):
    mesh_shape = tuple(mesh.shape[a] for a in AXES)
    placed = (P(None, "tile", None, "dp"), P("tile", None, "map"), P("tile", None))

    def run(frames, weights, offsets):
        return per_device(mesh_shape, frames, weights, offsets)

    return jax.shard_map(
        run,
        mesh=mesh,
        in_specs=placed,
        out_specs=(P("tile", "dp", "map"), P("tile", None, "map")),
        check_vma=False,
    )
```

```python
import functools

import jax
import jax.numpy as jnp
from jax import lax
from jax.experimental import pallas as pl
from jax.experimental.pallas import tpu as pltpu
from jax.sharding import PartitionSpec as P

FIELD = 18
POOL = 5
CORES = 2
STRIP = 48
SUB = 8
LANES = 128
MIB = 1 << 20
CUT_MIB = 50
OUT_ROWS = 2048

smoothing = 1.0
sparsity = 3.0
learn_rate = 0.1

AXES = ("tile", "map", "dp")
F32, BF16 = jnp.float32, jnp.bfloat16
VMEM = pl.BlockSpec(memory_space=pltpu.VMEM)
SMEM = pl.BlockSpec(memory_space=pltpu.SMEM)
ANY = pl.BlockSpec(memory_space=pl.ANY)
HBM = pl.BlockSpec(memory_space=pltpu.HBM)


def table(mesh_shape, move):
    tiles, maps, dps = mesh_shape
    rows_y = maps // CORES
    pairs = []
    for t in range(tiles):
        for y in range(rows_y):
            for k in range(CORES):
                for d in range(dps):
                    to = move(t, y, k, d)
                    if to is None or not 0 <= to[0] < tiles:
                        continue
                    t2, y2, k2, d2 = to
                    source = (t * maps + y * CORES + k) * dps + d
                    target = (t2 * maps + (y2 % rows_y) * CORES + k2) * dps + d2
                    pairs.append((source, target))
    return pairs


def params(mib):
    return pltpu.CompilerParams(vmem_limit_bytes=mib * MIB)


def cut_kernel(above, places, frames, *refs):
    out, token, strip, wide, flat, sems = refs[-6:]
    channels, rows_here, across, count = frames.shape
    column = lax.axis_index("map")
    top, left = places[0, column], places[1, column]
    base = jnp.minimum(left // 16 * 16, across - STRIP)
    base = pl.multiple_of(base, 16)
    first = jnp.minimum(top, rows_here - FIELD) if above else 0
    copies = [
        pltpu.make_async_copy(
            frames.at[channel, pl.ds(first, FIELD), pl.ds(base, STRIP), :],
            strip.at[channel],
            sems.at[channel],
        )
        for channel in range(channels)
    ]
    for copy in copies:
        copy.start()
    token[...] = jnp.zeros_like(token)
    shift = left - base
    for channel in range(channels):
        copies[channel].wait()
        for n in range(count // LANES):
            lanes = strip[channel, :, :, pl.ds(n * LANES, LANES)]
            wide[n] = lanes.reshape(FIELD * STRIP, LANES).astype(F32)
        for r in range(FIELD):
            row = top + r - (first if above else rows_here)
            valid = (row < FIELD) if above else (row >= 0)
            row = jnp.clip(row, 0, FIELD - 1)
            for n in range(count // LANES):
                x = wide[n, pl.ds(row * STRIP + shift, FIELD), :]
                x = jnp.where(valid, x, 0.0)
                at = pl.ds((channel * FIELD + r) * FIELD, FIELD)
                flat[at, pl.ds(n * LANES, LANES)] = x
    inner = channels * FIELD * FIELD
    out[...] = flat[pl.ds(0, inner), :].astype(BF16)


def cut(frames, places, above, after=()):
    channels, rows_here, wide, count = frames.shape
    inner = channels * FIELD * FIELD
    return pl.pallas_call(
        functools.partial(cut_kernel, above),
        out_shape=[
            jax.ShapeDtypeStruct((inner, count), BF16),
            jax.ShapeDtypeStruct((SUB, LANES), F32),
        ],
        in_specs=[SMEM, HBM] + [ANY] * len(after),
        out_specs=[VMEM] * 2,
        scratch_shapes=[
            pltpu.VMEM((channels, FIELD, STRIP, count), BF16),
            pltpu.VMEM((count // LANES, FIELD * STRIP, LANES), F32),
            pltpu.VMEM((inner, count), F32),
            pltpu.SemaphoreType.DMA((channels,)),
        ],
        compiler_params=params(CUT_MIB),
        name="cut_above" if above else "cut_below",
    )(places, frames, *after)


def blocks_kernel(rows_y, dps, flat, *refs):
    outs, wide = refs[-1 - rows_y : -1], refs[-1]
    inner = outs[0].shape[0]
    y, d = lax.axis_index("map") // CORES, lax.axis_index("dp")
    wide[...] = flat[...].astype(F32)
    for s in range(rows_y):
        column = dps * lax.rem(y + rows_y - s, rows_y) + d
        outs[s][...] = wide[pl.ds(column, inner, stride=rows_y * dps), :].astype(BF16)


def blocks(weights, rows_y, dps, after=()):
    num_cols, inner, here = weights.shape
    flat = weights.transpose(1, 0, 2).reshape(inner * num_cols, here)
    return pl.pallas_call(
        functools.partial(blocks_kernel, rows_y, dps),
        out_shape=[jax.ShapeDtypeStruct((inner, here), BF16)] * rows_y,
        in_specs=[VMEM] + [ANY] * len(after),
        out_specs=[VMEM] * rows_y,
        scratch_shapes=[pltpu.VMEM(flat.shape, F32)],
        compiler_params=params(16),
        name="blocks",
    )(flat, *after)


def filters_kernel(own, other, weight, turned):
    k = lax.rem(lax.axis_index("map"), CORES)
    for block, core in ((own[...], k), (other[...], 1 - k)):
        at = pl.multiple_of(core * LANES, LANES)
        weight[:, pl.ds(at, LANES)] = block
        turned[pl.ds(at, LANES), :] = block.T


def filters(own, other):
    inner, here = own.shape
    return pl.pallas_call(
        filters_kernel,
        out_shape=[
            jax.ShapeDtypeStruct((inner, CORES * here), BF16),
            jax.ShapeDtypeStruct((CORES * here, inner), BF16),
        ],
        in_specs=[VMEM] * 2,
        out_specs=[VMEM] * 2,
        compiler_params=params(8),
        name="filters",
    )(own, other)


def join_kernel(above, above_in, below, patch):
    mine = lax.rem(lax.axis_index("map"), CORES) == lax.axis_index("dp")

    @pl.when(mine)
    def _():
        patch[...] = above[...] + below[...]

    @pl.when(jnp.logical_not(mine))
    def _():
        patch[...] = above_in[...] + below[...]


def join(above, above_in, below):
    return pl.pallas_call(
        join_kernel,
        out_shape=jax.ShapeDtypeStruct(below.shape, BF16),
        in_specs=[VMEM] * 3,
        out_specs=VMEM,
        compiler_params=params(8),
        name="join",
    )(above, above_in, below)


def dot(a, b):
    return jnp.dot(a, b, preferred_element_type=F32)


def column_kernel(rows_y, patch_in, *refs):
    weight, turned = refs[:rows_y], refs[rows_y : 2 * rows_y]
    pe, mr, res, sq, inv = refs[2 * rows_y :]
    inner, count = patch_in.shape
    tile = weight[0].shape[1]
    maps = rows_y * tile
    pe[:, pl.ds(0, count)] = patch_in[...]
    patch = patch_in[...]
    for m in range(0, maps, tile):
        r = dot(turned[m // tile][...], patch)
        res[pl.ds(m, tile), :] = r
        mr[pl.ds(m, tile), pl.ds(count, count)] = r.astype(BF16)
        sq[pl.ds(m, tile), :] = r * r
    sq[pl.ds(maps, SUB), :] = sq[pl.ds(0, SUB), :]

    steps = -(-inner // tile)
    for n in range(steps):
        low, high = n * tile, min(inner, (n + 1) * tile)
        rows = pl.ds(low, high - low)
        error = -pe[rows, pl.ds(0, count)].astype(F32)
        for p in range(rows_y):
            error += dot(weight[p][rows, :], mr[pl.ds(p * tile, tile), pl.ds(count, count)])
        pe[rows, pl.ds(count, count)] = error.astype(BF16)
    for m in range(0, maps, tile):
        total = sq[pl.ds(m, tile), :]
        for i in range(1, POOL):
            total = total + sq[pl.ds(m + i, tile), :]
        inv[pl.ds(SUB + m, tile), :] = lax.rsqrt(smoothing + total)
    inv[pl.ds(0, SUB), :] = inv[pl.ds(maps, SUB), :]
    error_b = pe[:, pl.ds(count, count)]
    for m in range(0, maps, tile):
        back = dot(turned[m // tile][...], error_b)
        spread = inv[pl.ds(SUB + m, tile), :]
        for i in range(1, POOL):
            spread = spread + inv[pl.ds(SUB + m - i, tile), :]
        mixed = back + sparsity * res[pl.ds(m, tile), :] * spread
        mr[pl.ds(m, tile), pl.ds(0, count)] = mixed.astype(BF16)


def column(patch, weight, turned):
    inner, count = patch.shape
    rows_y = len(weight)
    maps = rows_y * weight[0].shape[1]
    return pl.pallas_call(
        functools.partial(column_kernel, rows_y),
        out_shape=[
            jax.ShapeDtypeStruct((inner, 2 * count), BF16),
            jax.ShapeDtypeStruct((maps, 2 * count), BF16),
        ],
        in_specs=[VMEM] * (1 + 2 * rows_y),
        out_specs=[VMEM] * 2,
        scratch_shapes=[
            pltpu.VMEM((maps, count), F32),
            pltpu.VMEM((maps + SUB, count), F32),
            pltpu.VMEM((maps + SUB, count), F32),
        ],
        compiler_params=params(40),
        name="column",
    )(patch, *weight, *turned)


def padded(rows):
    return -(-rows // 16) * 16


def piece_kernel(shifts, scale, pe, mr, *refs):
    home, away = refs[-2:]
    inner = pe.shape[0]
    first = lax.rem(lax.axis_index("map"), CORES) == 0
    tile = 256
    for i, p in enumerate(shifts):
        groups = mr[pl.ds(CORES * LANES * p, CORES * LANES), :]
        for n in range(0, inner, tile):
            size = min(tile, inner - n)
            g = lax.dot_general(
                pe[pl.ds(n, size), :], groups, (((1,), (1,)), ((), ())),
                preferred_element_type=F32,
            )
            g = g * scale
            low, high = g[:, :LANES], g[:, LANES:]
            rows = pl.ds(i * padded(inner) + n, size)
            home[rows, :] = jnp.where(first, low, high)
            away[rows, :] = jnp.where(first, high, low).astype(BF16)


def piece(shifts, pe, mr, after=()):
    inner, depth = pe.shape
    rows = len(shifts) * padded(inner)
    return pl.pallas_call(
        functools.partial(piece_kernel, shifts, 1.0 / depth),
        out_shape=[
            jax.ShapeDtypeStruct((rows, LANES), F32),
            jax.ShapeDtypeStruct((rows, LANES), BF16),
        ],
        in_specs=[VMEM] * 2 + [ANY] * len(after),
        out_specs=[VMEM] * 2,
        compiler_params=params(16),
        name="piece",
    )(pe, mr, *after)


def total_kernel(count, home, away, *refs):
    outs = refs[-count:]
    inner = outs[0].shape[0]
    for i, out in enumerate(outs):
        rows = pl.ds(i * padded(inner), inner)
        out[...] = (home[rows, :] + away[rows, :].astype(F32)).astype(BF16)


def total(home, away, count, inner, after):
    return pl.pallas_call(
        functools.partial(total_kernel, count),
        out_shape=[jax.ShapeDtypeStruct((inner, LANES), BF16)] * count,
        in_specs=[VMEM] * 2 + [ANY] * len(after),
        out_specs=[VMEM] * count,
        compiler_params=params(8),
        name="total",
    )(home, away, *after)


def follow_kernel(block, after, out):
    out[...] = block[...]


def follow(block, after):
    return pl.pallas_call(
        follow_kernel,
        out_shape=jax.ShapeDtypeStruct(block.shape, block.dtype),
        in_specs=[VMEM, ANY],
        out_specs=VMEM,
        compiler_params=params(4),
        name="follow",
    )(block, after)


def place_pieces(full, shifts, refs, rows_y, dps):
    y, d = lax.axis_index("map") // CORES, lax.axis_index("dp")
    inner = refs[0].shape[0]
    for n, s in enumerate(shifts):
        row = lax.rem(y + rows_y - s, rows_y)
        for block, part in ((refs[2 * n], d), (refs[2 * n + 1], 1 - d)):
            at = pl.ds(dps * row + part, inner, stride=rows_y * dps)
            full[at, :] = block[...].astype(F32)


def gather_kernel(rows_y, dps, shifts, *refs):
    place_pieces(refs[-1], shifts, refs[:-1], rows_y, dps)


def gather(pieces, shifts, rows_y, dps):
    inner, here = pieces[0].shape
    return pl.pallas_call(
        functools.partial(gather_kernel, rows_y, dps, shifts),
        out_shape=jax.ShapeDtypeStruct((inner * rows_y * dps, here), F32),
        in_specs=[VMEM] * len(pieces),
        out_specs=VMEM,
        compiler_params=params(8),
        name="gather",
    )(*pieces)


def finish_kernel(rows_y, dps, shifts, *refs):
    pieces, weights, early = refs[: 2 * len(shifts)], refs[-8], refs[-7]
    grad, fresh, full, new, grad_sem, sems = refs[-6:]
    full[...] = early[...]
    place_pieces(full, shifts, pieces, rows_y, dps)
    rows = full.shape[0]
    some = rows // dps
    at = pl.multiple_of(lax.axis_index("dp") * some, SUB)
    grad_copy = pltpu.make_async_copy(full.at[pl.ds(at, some), :], grad, grad_sem)
    grad_copy.start()
    copies = []
    for n, low in enumerate(range(0, rows, OUT_ROWS)):
        part = pl.ds(low, min(OUT_ROWS, rows - low))
        new[part, :] = (weights[part, :].astype(F32) - learn_rate * full[part, :]).astype(BF16)
        copy = pltpu.make_async_copy(new.at[part, :], fresh.at[part, :], sems.at[n])
        copy.start()
        copies.append(copy)
    grad_copy.wait()
    for copy in copies:
        copy.wait()


def finish(pieces, shifts, weights, full, rows_y, dps):
    num_cols, inner, here = weights.shape
    rows = inner * num_cols
    flat = weights.transpose(1, 0, 2).reshape(rows, here)
    grad, fresh = pl.pallas_call(
        functools.partial(finish_kernel, rows_y, dps, shifts),
        out_shape=[
            jax.ShapeDtypeStruct((rows // dps, here), F32),
            jax.ShapeDtypeStruct((rows, here), BF16),
        ],
        in_specs=[VMEM] * (len(pieces) + 2),
        out_specs=[HBM, HBM],
        scratch_shapes=[
            pltpu.VMEM((rows, here), F32),
            pltpu.VMEM((rows, here), BF16),
            pltpu.SemaphoreType.DMA,
            pltpu.SemaphoreType.DMA((-(-rows // OUT_ROWS),)),
        ],
        compiler_params=params(16),
        name="finish",
    )(*pieces, flat, full)
    grad = grad.reshape(inner // dps, num_cols, here).transpose(1, 0, 2)
    return grad, fresh.reshape(inner, num_cols, here).transpose(1, 0, 2)


def per_device(mesh_shape, frames, weights, offsets):
    rows_y = mesh_shape[1] // CORES
    def send(x, move):
        return lax.ppermute(x, AXES, table(mesh_shape, move))

    dps = mesh_shape[2]
    places = offsets.T
    upper = send(places, lambda t, y, k, d: (t + 1, y, k, d))
    above, token = cut(frames, places, True)
    below, token = cut(frames, upper, False, (token,))
    own = blocks(weights, rows_y, dps, (token,))
    below = send(below, lambda t, y, k, d: (t - 1, y, d, k))

    weight, turned = [], []
    for s in range(rows_y):
        block = own[s]
        if s:
            block = send(block, lambda t, y, k, d: (t, y - s, k, d))
        other = send(block, lambda t, y, k, d: (t, y, 1 - k, d))
        pair = filters(block, other)
        weight.append(pair[0])
        turned.append(pair[1])
    above_in = send(above, lambda t, y, k, d: (t, y, d, k) if k != d else None)

    pe, mr = column(join(above, above_in, below), weight, turned)

    pieces = {}
    inner = weights.shape[1]
    for s in (0, 1, 3, 2):
        home, away = piece((s,), pe, mr)
        away = send(away, lambda t, y, k, d: (t, y, 1 - k, d))
        (block,) = total(home, away, 1, inner, ())
        if s == 2:
            block = follow(block, pieces[1][0])
        if s:
            block = send(block, lambda t, y, k, d: (t, y + s, k, d))
        if s == 3:
            block = follow(block, pieces[0][1])
        pieces[s] = [block, send(block, lambda t, y, k, d: (t, y, k, 1 - d))]
    early, late = (0, 1, 3), (2,)
    full = gather(sum([pieces[s] for s in early], []), early, rows_y, dps)
    return finish(sum([pieces[s] for s in late], []), late, weights, full, rows_y, dps)


def solution(mesh):
    mesh_shape = tuple(mesh.shape[a] for a in AXES)
    placed = (P(None, "tile", None, "dp"), P("tile", None, "map"), P("tile", None))

    def run(frames, weights, offsets):
        return per_device(mesh_shape, frames, weights, offsets)

    return jax.shard_map(
        run,
        mesh=mesh,
        in_specs=placed,
        out_specs=(P("tile", "dp", "map"), P("tile", None, "map")),
        check_vma=False,
    )
```

```python
import functools

import jax
import jax.numpy as jnp
from jax import lax
from jax.experimental import pallas as pl
from jax.experimental.pallas import tpu as pltpu
from jax.sharding import PartitionSpec as P

FIELD = 18
POOL = 5
CORES = 2
STRIP = 48
SUB = 8
LANES = 128
MIB = 1 << 20
CUT_MIB = 50
FIRST = (0, 2, 1, 3)
OUT_ROWS = 2048

smoothing = 1.0
sparsity = 3.0
learn_rate = 0.1

AXES = ("tile", "map", "dp")
F32, BF16 = jnp.float32, jnp.bfloat16
VMEM = pl.BlockSpec(memory_space=pltpu.VMEM)
SMEM = pl.BlockSpec(memory_space=pltpu.SMEM)
ANY = pl.BlockSpec(memory_space=pl.ANY)
HBM = pl.BlockSpec(memory_space=pltpu.HBM)


def table(mesh_shape, move):
    tiles, maps, dps = mesh_shape
    rows_y = maps // CORES
    pairs = []
    for t in range(tiles):
        for y in range(rows_y):
            for k in range(CORES):
                for d in range(dps):
                    to = move(t, y, k, d)
                    if to is None or not 0 <= to[0] < tiles:
                        continue
                    t2, y2, k2, d2 = to
                    source = (t * maps + y * CORES + k) * dps + d
                    target = (t2 * maps + (y2 % rows_y) * CORES + k2) * dps + d2
                    pairs.append((source, target))
    return pairs


def params(mib):
    return pltpu.CompilerParams(vmem_limit_bytes=mib * MIB)


def cut_kernel(above, places, frames, *refs):
    out, token, strip, wide, flat, sems = refs[-6:]
    channels, rows_here, across, count = frames.shape
    column = lax.axis_index("map")
    top, left = places[0, column], places[1, column]
    base = jnp.minimum(left // 16 * 16, across - STRIP)
    base = pl.multiple_of(base, 16)
    first = jnp.minimum(top, rows_here - FIELD) if above else 0
    copies = [
        pltpu.make_async_copy(
            frames.at[channel, pl.ds(first, FIELD), pl.ds(base, STRIP), :],
            strip.at[channel],
            sems.at[channel],
        )
        for channel in range(channels)
    ]
    for copy in copies:
        copy.start()
    token[...] = jnp.zeros_like(token)
    shift = left - base
    for channel in range(channels):
        copies[channel].wait()
        for n in range(count // LANES):
            lanes = strip[channel, :, :, pl.ds(n * LANES, LANES)]
            wide[n] = lanes.reshape(FIELD * STRIP, LANES).astype(F32)
        for r in range(FIELD):
            row = top + r - (first if above else rows_here)
            valid = (row < FIELD) if above else (row >= 0)
            row = jnp.clip(row, 0, FIELD - 1)
            for n in range(count // LANES):
                x = wide[n, pl.ds(row * STRIP + shift, FIELD), :]
                x = jnp.where(valid, x, 0.0)
                at = pl.ds((channel * FIELD + r) * FIELD, FIELD)
                flat[at, pl.ds(n * LANES, LANES)] = x
    inner = channels * FIELD * FIELD
    out[...] = flat[pl.ds(0, inner), :].astype(BF16)


def cut(frames, places, above, after=()):
    channels, rows_here, wide, count = frames.shape
    inner = channels * FIELD * FIELD
    return pl.pallas_call(
        functools.partial(cut_kernel, above),
        out_shape=[
            jax.ShapeDtypeStruct((inner, count), BF16),
            jax.ShapeDtypeStruct((SUB, LANES), F32),
        ],
        in_specs=[SMEM, HBM] + [ANY] * len(after),
        out_specs=[VMEM] * 2,
        scratch_shapes=[
            pltpu.VMEM((channels, FIELD, STRIP, count), BF16),
            pltpu.VMEM((count // LANES, FIELD * STRIP, LANES), F32),
            pltpu.VMEM((inner, count), F32),
            pltpu.SemaphoreType.DMA((channels,)),
        ],
        compiler_params=params(CUT_MIB),
        name="cut_above" if above else "cut_below",
    )(places, frames, *after)


def blocks_kernel(rows_y, dps, flat, *refs):
    outs, wide = refs[-1 - rows_y : -1], refs[-1]
    inner = outs[0].shape[0]
    y, d = lax.axis_index("map") // CORES, lax.axis_index("dp")
    wide[...] = flat[...].astype(F32)
    for s in range(rows_y):
        column = dps * lax.rem(y + rows_y - s, rows_y) + d
        outs[s][...] = wide[pl.ds(column, inner, stride=rows_y * dps), :].astype(BF16)


def blocks(weights, rows_y, dps, after=()):
    num_cols, inner, here = weights.shape
    flat = weights.transpose(1, 0, 2).reshape(inner * num_cols, here)
    return pl.pallas_call(
        functools.partial(blocks_kernel, rows_y, dps),
        out_shape=[jax.ShapeDtypeStruct((inner, here), BF16)] * rows_y,
        in_specs=[VMEM] + [ANY] * len(after),
        out_specs=[VMEM] * rows_y,
        scratch_shapes=[pltpu.VMEM(flat.shape, F32)],
        compiler_params=params(16),
        name="blocks",
    )(flat, *after)


def filters_kernel(own, other, weight, turned):
    k = lax.rem(lax.axis_index("map"), CORES)
    for block, core in ((own[...], k), (other[...], 1 - k)):
        at = pl.multiple_of(core * LANES, LANES)
        weight[:, pl.ds(at, LANES)] = block
        turned[pl.ds(at, LANES), :] = block.T


def filters(own, other):
    inner, here = own.shape
    return pl.pallas_call(
        filters_kernel,
        out_shape=[
            jax.ShapeDtypeStruct((inner, CORES * here), BF16),
            jax.ShapeDtypeStruct((CORES * here, inner), BF16),
        ],
        in_specs=[VMEM] * 2,
        out_specs=[VMEM] * 2,
        compiler_params=params(8),
        name="filters",
    )(own, other)


def join_kernel(above, above_in, below, patch):
    mine = lax.rem(lax.axis_index("map"), CORES) == lax.axis_index("dp")

    @pl.when(mine)
    def _():
        patch[...] = above[...] + below[...]

    @pl.when(jnp.logical_not(mine))
    def _():
        patch[...] = above_in[...] + below[...]


def join(above, above_in, below):
    return pl.pallas_call(
        join_kernel,
        out_shape=jax.ShapeDtypeStruct(below.shape, BF16),
        in_specs=[VMEM] * 3,
        out_specs=VMEM,
        compiler_params=params(8),
        name="join",
    )(above, above_in, below)


def dot(a, b):
    return jnp.dot(a, b, preferred_element_type=F32)


def column_kernel(rows_y, patch_in, *refs):
    weight = [refs[p] for p in FIRST]
    turned = [refs[rows_y + p] for p in FIRST]
    pe, mr, res, sq, inv = refs[2 * rows_y :]
    inner, count = patch_in.shape
    tile = weight[0].shape[1]
    maps = rows_y * tile
    pe[:, pl.ds(0, count)] = patch_in[...]
    patch = patch_in[...]
    for m in range(0, maps, tile):
        r = dot(turned[m // tile][...], patch)
        res[pl.ds(m, tile), :] = r
        mr[pl.ds(m, tile), pl.ds(count, count)] = r.astype(BF16)
        sq[pl.ds(m, tile), :] = r * r
    sq[pl.ds(maps, SUB), :] = sq[pl.ds(0, SUB), :]

    steps = -(-inner // tile)
    for n in range(steps):
        low, high = n * tile, min(inner, (n + 1) * tile)
        rows = pl.ds(low, high - low)
        error = -pe[rows, pl.ds(0, count)].astype(F32)
        for p in range(rows_y):
            error += dot(weight[p][rows, :], mr[pl.ds(p * tile, tile), pl.ds(count, count)])
        pe[rows, pl.ds(count, count)] = error.astype(BF16)
    for m in range(0, maps, tile):
        total = sq[pl.ds(m, tile), :]
        for i in range(1, POOL):
            total = total + sq[pl.ds(m + i, tile), :]
        inv[pl.ds(SUB + m, tile), :] = lax.rsqrt(smoothing + total)
    inv[pl.ds(0, SUB), :] = inv[pl.ds(maps, SUB), :]
    error_b = pe[:, pl.ds(count, count)]
    for m in range(0, maps, tile):
        back = dot(turned[m // tile][...], error_b)
        spread = inv[pl.ds(SUB + m, tile), :]
        for i in range(1, POOL):
            spread = spread + inv[pl.ds(SUB + m - i, tile), :]
        mixed = back + sparsity * res[pl.ds(m, tile), :] * spread
        mr[pl.ds(m, tile), pl.ds(0, count)] = mixed.astype(BF16)


def column(patch, weight, turned):
    inner, count = patch.shape
    rows_y = len(weight)
    maps = rows_y * weight[0].shape[1]
    return pl.pallas_call(
        functools.partial(column_kernel, rows_y),
        out_shape=[
            jax.ShapeDtypeStruct((inner, 2 * count), BF16),
            jax.ShapeDtypeStruct((maps, 2 * count), BF16),
        ],
        in_specs=[VMEM] * (1 + 2 * rows_y),
        out_specs=[VMEM] * 2,
        scratch_shapes=[
            pltpu.VMEM((maps, count), F32),
            pltpu.VMEM((maps + SUB, count), F32),
            pltpu.VMEM((maps + SUB, count), F32),
        ],
        compiler_params=params(40),
        name="column",
    )(patch, *[weight[p] for p in FIRST], *[turned[p] for p in FIRST])


def padded(rows):
    return -(-rows // 16) * 16


def piece_kernel(shifts, scale, pe, mr, *refs):
    home, away = refs[-2:]
    inner = pe.shape[0]
    first = lax.rem(lax.axis_index("map"), CORES) == 0
    tile = 256
    for i, p in enumerate(shifts):
        groups = mr[pl.ds(CORES * LANES * p, CORES * LANES), :]
        for n in range(0, inner, tile):
            size = min(tile, inner - n)
            g = lax.dot_general(
                pe[pl.ds(n, size), :], groups, (((1,), (1,)), ((), ())),
                preferred_element_type=F32,
            )
            g = g * scale
            low, high = g[:, :LANES], g[:, LANES:]
            rows = pl.ds(i * padded(inner) + n, size)
            home[rows, :] = jnp.where(first, low, high)
            away[rows, :] = jnp.where(first, high, low).astype(BF16)


def piece(shifts, pe, mr, after=()):
    inner, depth = pe.shape
    rows = len(shifts) * padded(inner)
    return pl.pallas_call(
        functools.partial(piece_kernel, shifts, 1.0 / depth),
        out_shape=[
            jax.ShapeDtypeStruct((rows, LANES), F32),
            jax.ShapeDtypeStruct((rows, LANES), BF16),
        ],
        in_specs=[VMEM] * 2 + [ANY] * len(after),
        out_specs=[VMEM] * 2,
        compiler_params=params(16),
        name="piece",
    )(pe, mr, *after)


def total_kernel(count, home, away, *refs):
    outs = refs[-count:]
    inner = outs[0].shape[0]
    for i, out in enumerate(outs):
        rows = pl.ds(i * padded(inner), inner)
        out[...] = (home[rows, :] + away[rows, :].astype(F32)).astype(BF16)


def total(home, away, count, inner, after):
    return pl.pallas_call(
        functools.partial(total_kernel, count),
        out_shape=[jax.ShapeDtypeStruct((inner, LANES), BF16)] * count,
        in_specs=[VMEM] * 2 + [ANY] * len(after),
        out_specs=[VMEM] * count,
        compiler_params=params(8),
        name="total",
    )(home, away, *after)


def follow_kernel(block, after, out):
    out[...] = block[...]


def follow(block, after):
    return pl.pallas_call(
        follow_kernel,
        out_shape=jax.ShapeDtypeStruct(block.shape, block.dtype),
        in_specs=[VMEM, ANY],
        out_specs=VMEM,
        compiler_params=params(4),
        name="follow",
    )(block, after)


def place_pieces(full, shifts, refs, rows_y, dps):
    y, d = lax.axis_index("map") // CORES, lax.axis_index("dp")
    inner = refs[0].shape[0]
    for n, s in enumerate(shifts):
        row = lax.rem(y + rows_y - s, rows_y)
        for block, part in ((refs[2 * n], d), (refs[2 * n + 1], 1 - d)):
            at = pl.ds(dps * row + part, inner, stride=rows_y * dps)
            full[at, :] = block[...].astype(F32)


def gather_kernel(rows_y, dps, shifts, *refs):
    place_pieces(refs[-1], shifts, refs[:-1], rows_y, dps)


def gather(pieces, shifts, rows_y, dps):
    inner, here = pieces[0].shape
    return pl.pallas_call(
        functools.partial(gather_kernel, rows_y, dps, shifts),
        out_shape=jax.ShapeDtypeStruct((inner * rows_y * dps, here), F32),
        in_specs=[VMEM] * len(pieces),
        out_specs=VMEM,
        compiler_params=params(8),
        name="gather",
    )(*pieces)


def finish_kernel(rows_y, dps, shifts, *refs):
    pieces, weights, early = refs[: 2 * len(shifts)], refs[-8], refs[-7]
    grad, fresh, full, new, grad_sem, sems = refs[-6:]
    full[...] = early[...]
    place_pieces(full, shifts, pieces, rows_y, dps)
    rows = full.shape[0]
    some = rows // dps
    at = pl.multiple_of(lax.axis_index("dp") * some, SUB)
    grad_copy = pltpu.make_async_copy(full.at[pl.ds(at, some), :], grad, grad_sem)
    grad_copy.start()
    copies = []
    for n, low in enumerate(range(0, rows, OUT_ROWS)):
        part = pl.ds(low, min(OUT_ROWS, rows - low))
        new[part, :] = (weights[part, :].astype(F32) - learn_rate * full[part, :]).astype(BF16)
        copy = pltpu.make_async_copy(new.at[part, :], fresh.at[part, :], sems.at[n])
        copy.start()
        copies.append(copy)
    grad_copy.wait()
    for copy in copies:
        copy.wait()


def finish(pieces, shifts, weights, full, rows_y, dps):
    num_cols, inner, here = weights.shape
    rows = inner * num_cols
    flat = weights.transpose(1, 0, 2).reshape(rows, here)
    grad, fresh = pl.pallas_call(
        functools.partial(finish_kernel, rows_y, dps, shifts),
        out_shape=[
            jax.ShapeDtypeStruct((rows // dps, here), F32),
            jax.ShapeDtypeStruct((rows, here), BF16),
        ],
        in_specs=[VMEM] * (len(pieces) + 2),
        out_specs=[HBM, HBM],
        scratch_shapes=[
            pltpu.VMEM((rows, here), F32),
            pltpu.VMEM((rows, here), BF16),
            pltpu.SemaphoreType.DMA,
            pltpu.SemaphoreType.DMA((-(-rows // OUT_ROWS),)),
        ],
        compiler_params=params(16),
        name="finish",
    )(*pieces, flat, full)
    grad = grad.reshape(inner // dps, num_cols, here).transpose(1, 0, 2)
    return grad, fresh.reshape(inner, num_cols, here).transpose(1, 0, 2)


def per_device(mesh_shape, frames, weights, offsets):
    rows_y = mesh_shape[1] // CORES
    def send(x, move):
        return lax.ppermute(x, AXES, table(mesh_shape, move))

    dps = mesh_shape[2]
    places = offsets.T
    upper = send(places, lambda t, y, k, d: (t + 1, y, k, d))
    above, token = cut(frames, places, True)
    below, token = cut(frames, upper, False, (token,))
    own = blocks(weights, rows_y, dps, (token,))
    below = send(below, lambda t, y, k, d: (t - 1, y, d, k))

    pairs = {}
    for s in FIRST:
        block = own[s]
        if s:
            block = send(block, lambda t, y, k, d: (t, y - s, k, d))
        other = send(block, lambda t, y, k, d: (t, y, 1 - k, d))
        pairs[s] = filters(block, other)
    weight, turned = zip(*(pairs[s] for s in range(rows_y)))
    above_in = send(above, lambda t, y, k, d: (t, y, d, k) if k != d else None)

    pe, mr = column(join(above, above_in, below), weight, turned)

    pieces = {}
    inner = weights.shape[1]
    for s in (0, 1, 3, 2):
        home, away = piece((s,), pe, mr)
        away = send(away, lambda t, y, k, d: (t, y, 1 - k, d))
        (block,) = total(home, away, 1, inner, ())
        if s == 2:
            block = follow(block, pieces[0][1])
        if s:
            block = send(block, lambda t, y, k, d: (t, y + s, k, d))
        pieces[s] = [block, send(block, lambda t, y, k, d: (t, y, k, 1 - d))]
    early, late = (0, 1, 3), (2,)
    full = gather(sum([pieces[s] for s in early], []), early, rows_y, dps)
    return finish(sum([pieces[s] for s in late], []), late, weights, full, rows_y, dps)


def solution(mesh):
    mesh_shape = tuple(mesh.shape[a] for a in AXES)
    placed = (P(None, "tile", None, "dp"), P("tile", None, "map"), P("tile", None))

    def run(frames, weights, offsets):
        return per_device(mesh_shape, frames, weights, offsets)

    return jax.shard_map(
        run,
        mesh=mesh,
        in_specs=placed,
        out_specs=(P("tile", "dp", "map"), P("tile", None, "map")),
        check_vma=False,
    )
```
